128 devices in a mesh: seq: 16 (over z, y), exp: 8 (over x, core).
Axes of the slice: x: 4, y: 4, z: 4, core: 2. Of those that a mesh axis runs over, the one named last changes fastest.
Arguments:
- tokens: bfloat16 [8192, 2048], P('seq', 'exp'), may hold values from -6 to 6
- grad_out: bfloat16 [8192, 2048], P('seq', 'exp'), may hold values from -6 to 6
- chosen: int32 [16, 512], replicated, may hold values from 0 to 8191, as said below
- scores: float32 [16, 512], P('seq'), may hold values from 0.2 to 2
- gate_weight: bfloat16 [16, 2048, 8192], P('seq', None, 'exp'), may hold values from -0.125 to 0.125
- up_weight: bfloat16 [16, 2048, 8192], P('seq', None, 'exp'), may hold values from -0.125 to 0.125
- down_weight: bfloat16 [16, 8192, 2048], P('seq', 'exp'), may hold values from -0.0625 to 0.0625
Outputs:
- grad_tokens: bfloat16 [8192, 2048], P('seq', 'exp')
- grad_scores: float32 [16, 512], P('seq')
- grad_gate: bfloat16 [16, 2048, 8192], P('seq', None, 'exp')
- grad_up: bfloat16 [16, 2048, 8192], P('seq', None, 'exp')
- grad_down: bfloat16 [16, 8192, 2048], P('seq', 'exp')
The draws below stay inside these ranges and needn't reach their ends.
Inputs may be any that keep to these rules, and one draw needn't show every extreme that they name: `chosen`: each row holds 512 distinct token indices in ascending order. For every expert and every owner o (tokens o * 512 to (o + 1) * 512 - 1) at most 64 of its indices lie with o, and exactly 64 for some owner of every expert.
All inputs are finite; a program needn't handle non-finite values.
Results may differ from the reference program's by a relative error of at most 0.007.
Values may be sent and summed in bfloat16 or wider, within the bound.
A program may use at most 128 MiB of HBM per device.

```python
import math
import jax
import jax.numpy as jnp
from jax import lax

D = 2048
H = 8192
CAP = 512
TOK_DEV = 512
TOKENS = 8192
EXPERTS = 16


def draw_chosen(key, part):
    key = jax.random.fold_in(key, 7)
    key_rank, key_pairs, key_pick = jax.random.split(key, 3)
    owners = TOKENS // TOK_DEV
    middle = CAP // owners
    ranking = jax.random.permutation(key_rank, owners)

    def counts_for(inner):
        key_perm, key_amount = jax.random.split(inner)
        order = jax.random.permutation(key_perm, owners)
        amount = jax.random.randint(key_amount, (owners // 2,), 0, middle + 1)
        amount = amount.at[0].set(middle)
        left = order[0::2]
        right = order[1::2]
        left_hot = ranking[left] > ranking[right]
        counts = jnp.zeros((owners,), jnp.int32)
        counts = counts.at[left].set(jnp.where(left_hot, middle + amount, middle - amount))
        counts = counts.at[right].set(jnp.where(left_hot, middle - amount, middle + amount))
        return counts
    counts = jax.vmap(counts_for)(jax.random.split(key_pairs, EXPERTS))
    rough = jax.random.randint(key_pick, (EXPERTS, owners, TOK_DEV), 0, 1 << 20)
    ranked = rough * TOK_DEV + jnp.arange(TOK_DEV, dtype=jnp.int32)[None, None, :]
    places = jnp.argsort(jnp.argsort(ranked, axis=2), axis=2)
    marked = (places < counts[:, :, None]).reshape(EXPERTS, TOKENS)

    def listed(flags):
        return jnp.nonzero(flags, size=CAP)[0].astype(jnp.int32)
    return jax.vmap(listed)(marked)


def block_levels(key, extent, cuts, smallest, high):
    def one(axis_at, parts):
        heights = jax.random.uniform(jax.random.fold_in(jax.random.fold_in(key, 6), axis_at), (parts,), jnp.float32, smallest / len(cuts), high / len(cuts))
        return jnp.repeat(jnp.exp(heights), extent[axis_at] // parts).reshape((-1,) + (1,) * (len(extent) - axis_at - 1))

    factor_of = one(*cuts[0])
    for cut in cuts[1:]:
        factor_of = factor_of * one(*cut)
    return factor_of


def gaussian(key, extent, width, limit, pieces=(), kind=jnp.bfloat16):
    loudness = block_levels(key, extent, pieces, -0.22, 0.18) if pieces else 1.0
    array = jax.random.normal(key, extent, jnp.float32) * width * loudness
    return jnp.minimum(jnp.maximum(array, -limit), limit).astype(kind)


def setup_inputs(seed: int = 0) -> dict:
    key_of = jax.random.split(jax.random.key(seed), 8)
    return {
        "tokens": gaussian(key_of[0], (TOKENS, D), 1.0, 6.0, ((0, 16), (1, 8))),
        "grad_out": gaussian(key_of[1], (TOKENS, D), 1.0, 6.0, ((0, 16), (1, 8))),
        "chosen": draw_chosen(jax.random.fold_in(key_of[7], 71), 0),
        "scores": jnp.clip(jnp.exp(math.log(2.0) - 2.3025851 * jax.random.uniform(key_of[3], (EXPERTS, CAP), jnp.float32) ** block_levels(key_of[3], (EXPERTS, CAP), ((0, 16),), -0.2, 0.2)), 0.2, 2.0),
        "gate_weight": gaussian(key_of[4], (EXPERTS, D, H), D ** -0.5, 0.125, ((0, 16), (2, 8))),
        "up_weight": gaussian(key_of[5], (EXPERTS, D, H), D ** -0.5, 0.125, ((0, 16), (2, 8))),
        "down_weight": gaussian(key_of[6], (EXPERTS, H, D), H ** -0.5, 0.0625, ((0, 16), (1, 8))),
    }


def expert_backward(rows, grads, gains, gate_mat, up_mat, down_mat):
    gate_pre = jnp.dot(rows, gate_mat, preferred_element_type=jnp.float32)
    up_pre = jnp.dot(rows, up_mat, preferred_element_type=jnp.float32)
    sigma = jax.nn.sigmoid(gate_pre)
    silu_gate = gate_pre * sigma
    hidden = (silu_gate * up_pre).astype(jnp.bfloat16)
    back_hidden = lax.dot_general(grads, down_mat, (((1,), (1,)), ((), ())), preferred_element_type=jnp.float32)
    score_grad = jnp.sum(hidden.astype(jnp.float32) * back_hidden, axis=1)
    scaled = (gains[:, None] * grads.astype(jnp.float32)).astype(jnp.bfloat16)
    grad_down = lax.dot_general(hidden, scaled, (((0,), (0,)), ((), ())), preferred_element_type=jnp.float32).astype(jnp.bfloat16)
    hidden_grad = gains[:, None] * back_hidden
    grad_gate_pre = (hidden_grad * up_pre * sigma * (1.0 + gate_pre * (1.0 - sigma))).astype(jnp.bfloat16)
    grad_up_pre = (hidden_grad * silu_gate).astype(jnp.bfloat16)
    grad_gate = lax.dot_general(rows, grad_gate_pre, (((0,), (0,)), ((), ())), preferred_element_type=jnp.float32).astype(jnp.bfloat16)
    grad_up = lax.dot_general(rows, grad_up_pre, (((0,), (0,)), ((), ())), preferred_element_type=jnp.float32).astype(jnp.bfloat16)
    partial_value = lax.dot_general(grad_gate_pre, gate_mat, (((1,), (1,)), ((), ())), preferred_element_type=jnp.float32)
    partial_value = partial_value + lax.dot_general(grad_up_pre, up_mat, (((1,), (1,)), ((), ())), preferred_element_type=jnp.float32)
    return score_grad, grad_gate, grad_up, grad_down, partial_value


def reference(tokens, grad_out, chosen, scores, gate_weight, up_weight, down_weight):
    def step(carry, expert):
        positions = chosen[expert].astype(jnp.int32)
        rows = tokens[positions]
        grads = grad_out[positions]
        score_grad, grad_gate, grad_up, grad_down, partial_value = expert_backward(
            rows, grads, scores[expert], gate_weight[expert], up_weight[expert], down_weight[expert])
        contrib = lax.optimization_barrier(partial_value.astype(jnp.bfloat16)).astype(jnp.float32)
        carry = carry.at[positions].add(contrib)
        return carry, (score_grad, grad_gate, grad_up, grad_down)

    start = jnp.zeros(tokens.shape, jnp.float32)
    total, stacked = lax.scan(step, start, jnp.arange(EXPERTS, dtype=jnp.int32))
    grad_scores, grad_gate, grad_up, grad_down = stacked
    return total.astype(jnp.bfloat16), grad_scores, grad_gate, grad_up, grad_down
```

```python
import jax
import jax.numpy as jnp
from jax import lax
from jax.sharding import PartitionSpec as P


def send_matrix(chosen, owner_id, tok_dev, most):
    experts, width = chosen.shape
    lower = owner_id * tok_dev
    mine = (chosen >= lower) & (chosen < lower + tok_dev)
    begins = jnp.sum(chosen < lower, axis=1)
    rank = jnp.arange(width, dtype=jnp.int32)[None, :] - begins[:, None]
    slot = jnp.where(mine, rank, -1)
    hit = slot[:, None, :] == jnp.arange(most, dtype=jnp.int32)[None, :, None]
    token = jnp.sum(jnp.where(hit, chosen[:, None, :] - lower + 1, 0), axis=2) - 1
    flat = token.reshape(experts * most, 1)
    return (flat == jnp.arange(tok_dev, dtype=jnp.int32)[None, :]).astype(jnp.bfloat16)


def pick_matrix(picked, owners, tok_dev, most):
    width = picked.shape[0]
    bounds = jnp.arange(owners, dtype=jnp.int32) * tok_dev
    begins = jnp.sum(picked[None, :] < bounds[:, None], axis=1)
    source = picked // tok_dev
    onehot = source[None, :] == jnp.arange(owners, dtype=jnp.int32)[:, None]
    first = jnp.sum(jnp.where(onehot, begins[:, None], 0), axis=0)
    flat = source * most + jnp.arange(width, dtype=jnp.int32) - first
    return (jnp.arange(owners * most, dtype=jnp.int32)[:, None] == flat[None, :]).astype(jnp.bfloat16)


def dot(a, b, ca, cb):
    return lax.dot_general(a, b, (((ca,), (cb,)), ((), ())), preferred_element_type=jnp.float32)


def shards(tokens, grad_out, chosen, scores, gate_weight, up_weight, down_weight):
    owner_id = lax.axis_index("seq")
    owners = lax.axis_size("seq")
    tok_dev, part = tokens.shape
    width = chosen.shape[1]
    most = 2 * width // owners
    bf16 = jnp.bfloat16
    send = send_matrix(chosen, owner_id, tok_dev, most)
    both = jnp.concatenate([tokens, grad_out], axis=1)
    out = dot(send, both, 1, 0).astype(bf16).reshape(owners, most, 2 * part)
    recv = lax.all_to_all(out, "seq", split_axis=0, concat_axis=0, tiled=True)
    picked = lax.dynamic_index_in_dim(chosen, owner_id, 0, keepdims=False)
    pick = pick_matrix(picked, owners, tok_dev, most)
    mine = dot(pick, recv.reshape(owners * most, 2 * part), 0, 0).astype(bf16)
    rows = lax.all_gather(mine[:, :part], "exp", axis=1, tiled=True)
    grads = lax.all_gather(mine[:, part:], "exp", axis=1, tiled=True)
    gains = scores[0]
    gate_mat = gate_weight[0]
    up_mat = up_weight[0]
    down_mat = down_weight[0]
    gate_pre = dot(rows, gate_mat, 1, 0)
    up_pre = dot(rows, up_mat, 1, 0)
    sigma = jax.nn.sigmoid(gate_pre)
    silu_gate = gate_pre * sigma
    hidden = (silu_gate * up_pre).astype(bf16)
    back_hidden = dot(grads, down_mat, 1, 1)
    score_part = jnp.sum(hidden.astype(jnp.float32) * back_hidden, axis=1)
    grad_scores = lax.psum(score_part, "exp")
    scaled = (gains[:, None] * grads.astype(jnp.float32)).astype(bf16)
    hidden_grad = gains[:, None] * back_hidden
    grad_gate_pre = (hidden_grad * up_pre * sigma * (1.0 + gate_pre * (1.0 - sigma))).astype(bf16)
    grad_up_pre = (hidden_grad * silu_gate).astype(bf16)
    partial_value = (dot(grad_gate_pre, gate_mat, 1, 1) + dot(grad_up_pre, up_mat, 1, 1)).astype(bf16)
    summed = lax.psum_scatter(partial_value, "exp", scatter_dimension=1, tiled=True)
    grad_down = dot(hidden, scaled, 0, 0).astype(bf16)
    grad_gate = dot(rows, grad_gate_pre, 0, 0).astype(bf16)
    grad_up = dot(rows, grad_up_pre, 0, 0).astype(bf16)
    outgoing = dot(pick, summed, 1, 0).astype(bf16).reshape(owners, most, part)
    returned = lax.all_to_all(outgoing, "seq", split_axis=0, concat_axis=0, tiled=True)
    total = dot(send, returned.reshape(owners * most, part), 0, 0)
    return (
        total.astype(bf16),
        grad_scores[None, :],
        grad_gate[None],
        grad_up[None],
        grad_down[None],
    )


def solution(mesh):
    in_specs = (
        P("seq", "exp"),
        P("seq", "exp"),
        P(),
        P("seq", None),
        P("seq", None, "exp"),
        P("seq", None, "exp"),
        P("seq", "exp", None),
    )
    out_specs = (
        P("seq", "exp"),
        P("seq", None),
        P("seq", None, "exp"),
        P("seq", None, "exp"),
        P("seq", "exp", None),
    )
    return jax.shard_map(shards, mesh=mesh, in_specs=in_specs, out_specs=out_specs, check_vma=False)
```

```python
import functools

import jax
import jax.numpy as jnp
from jax import lax
from jax.experimental import pallas as pl
from jax.experimental.pallas import tpu as pltpu
from jax.sharding import PartitionSpec as P

MESH = pl.DeviceIdType.MESH
BF16 = jnp.bfloat16
F32 = jnp.float32

OWNERS = 16
MOST = 64
CAP = 512
PART = 256
CHIPS = 4
WIDE = 512
HID = 1024
HALF = CAP // 2
VMEM_BYTES = 60 * 1024 * 1024


def dot(a, b):
    return jnp.dot(a, b, preferred_element_type=F32)


def dot_t(a, b):
    return lax.dot_general(a, b, (((1,), (1,)), ((), ())), preferred_element_type=F32)


def iota(shape, axis):
    return lax.broadcasted_iota(jnp.int32, shape, axis)


def part_of(c):
    return pl.ds(pl.multiple_of(c * PART, PART), PART)


def layer_kernel(
    tokens, grads_in, chosen, scores, gate_hbm, up_hbm, down_hbm,
    tok_out, score_out, rows_t_hbm, scaled_hbm, hidden_t_hbm, ggp_hbm, gup_hbm,
    gate_v, up_v, down_v, full, gate_acc, up_acc, back_acc, hidden, hidden_t, ggp, gup,
    rows_t, send_m, send_t, pick_m, pick_t, out_x, in_x, out_r, in_r, sums, sib_out, sib_in,
    rel_out, rel_in, dir_out, dir_in, fin_out, fin_in, score_buf, gain_col,
    w_sem, o_sem, x_send, x_recv, g_send, g_recv, s_send, s_recv, c_send, c_recv, r_send, r_recv,
    q_send, q_recv,
):
    seq = lax.axis_index("seq")
    ex = lax.axis_index("exp")
    zz, yy = seq // 4, lax.rem(seq, 4)
    x, c = ex // 2, lax.rem(ex, 2)
    right, left, opp = lax.rem(x + 1, 4), lax.rem(x + 3, 4), lax.rem(x + 2, 4)
    oc = 1 - c

    def seq_peer(k):
        dz, dy = k // 4, lax.rem(k, 4)
        return lax.rem(zz + dz, 4) * 4 + lax.rem(yy + dy, 4)

    weight_copies = [
        pltpu.make_async_copy(gate_hbm, gate_v, w_sem.at[0]),
        pltpu.make_async_copy(up_hbm, up_v, w_sem.at[1]),
    ] + [
        pltpu.make_async_copy(down_hbm.at[0, :, pl.ds(i * WIDE, WIDE)], down_v.at[i], w_sem.at[2 + i])
        for i in range(CHIPS)
    ]
    for copy in weight_copies:
        copy.start()

    barrier = pltpu.get_barrier_semaphore()

    def greet_seq(k, carry):
        pl.semaphore_signal(barrier, inc=1, device_id=(seq_peer(k), ex), device_id_type=MESH)
        return carry

    def greet_exp(k, carry):
        pl.semaphore_signal(barrier, inc=1, device_id=(seq, lax.rem(ex + k, 8)), device_id_type=MESH)
        return carry

    lax.fori_loop(1, OWNERS, greet_seq, 0)
    lax.fori_loop(1, 8, greet_exp, 0)

    lane = iota((1, CAP), 1)
    lower = seq * CAP
    table = chosen[...]
    begins = jnp.sum((table < lower).astype(jnp.int32), axis=1, keepdims=True)
    mine = jnp.logical_and(table >= lower, table < lower + CAP)
    slots = jnp.where(mine, iota((OWNERS, CAP), 1) - begins, -1)
    local = table - lower
    sub = iota((MOST, CAP), 0)
    lanes = iota((MOST, CAP), 1)
    for e in range(OWNERS):
        hit = slots[e : e + 1, :] == sub
        token = jnp.sum(jnp.where(hit, local[e : e + 1, :] + 1, 0), axis=1, keepdims=True) - 1
        send_m[e * MOST : (e + 1) * MOST, :] = jnp.where(token == lanes, 1.0, 0.0).astype(BF16)
    out_x[0] = dot(send_m[...], tokens[...]).astype(BF16)

    def x_copy(a, peer, slot):
        return pltpu.make_async_remote_copy(
            src_ref=out_x.at[a, pl.ds(pl.multiple_of(peer * MOST, MOST), MOST), :],
            dst_ref=in_x.at[a, pl.ds(pl.multiple_of(slot * MOST, MOST), MOST), :],
            send_sem=x_send.at[a, peer],
            recv_sem=x_recv.at[a, slot],
            device_id=(peer, ex),
            device_id_type=MESH,
        )

    def x_start(a):
        def body(k, carry):
            x_copy(a, seq_peer(k), seq).start()
            return carry

        lax.fori_loop(1, OWNERS, body, 0)
        here = pl.ds(pl.multiple_of(seq * MOST, MOST), MOST)
        in_x[a, here, :] = out_x[a, here, :]

    def x_wait(a):
        def body(k, carry):
            peer = seq_peer(k)
            x_copy(a, peer, peer).wait_recv()
            return carry

        lax.fori_loop(1, OWNERS, body, 0)

    pl.semaphore_wait(barrier, OWNERS - 1 + 7)
    x_start(0)
    out_x[1] = dot(send_m[...], grads_in[...]).astype(BF16)
    x_start(1)

    picked = chosen[pl.ds(seq, 1), :]
    owner_low = iota((OWNERS, CAP), 0) * CAP
    wide = jnp.broadcast_to(picked, (OWNERS, CAP))
    firsts = jnp.sum((wide < owner_low).astype(jnp.int32), axis=1, keepdims=True)
    inside = jnp.logical_and(wide >= owner_low, wide < owner_low + CAP)
    places = jnp.where(inside, iota((OWNERS, CAP), 1) - firsts, -1)
    for g in range(OWNERS // 2):
        block = jnp.concatenate(
            [jnp.where(places[o : o + 1, :] == sub, 1.0, 0.0) for o in (2 * g, 2 * g + 1)], axis=0
        )
        here = slice(g * 2 * MOST, (g + 1) * 2 * MOST)
        pick_t[here, :] = block.astype(BF16)
        pick_m[:, here] = block.T.astype(BF16)
    gain_col[...] = jnp.broadcast_to(scores[...], (128, CAP)).T

    def piece(a, xx, cc, half=None):
        rows = slice(None) if half is None else pl.ds(half * HALF, HALF)
        return full.at[a, xx, rows, part_of(cc)]

    def g_copy(a, k):
        view, target = {
            0: (piece(a, x, c), (x, oc)),
            1: (piece(a, x, c), (right, c)),
            2: (piece(a, x, c), (left, c)),
            3: (piece(a, left, c), (x, oc)),
            4: (piece(a, right, c), (x, oc)),
            5: (piece(a, left, c, 0), (right, c)),
            6: (piece(a, right, c, 1), (left, c)),
            7: (piece(a, opp, c, 0), (x, oc)),
            8: (piece(a, opp, c, 1), (x, oc)),
        }[k]
        return pltpu.make_async_remote_copy(
            src_ref=view, dst_ref=view, send_sem=g_send.at[a, k], recv_sem=g_recv.at[a, k],
            device_id=(seq, target[0] * 2 + target[1]), device_id_type=MESH,
        )

    def g_wait(a, *ks):
        for k in ks:
            g_copy(a, k).wait_recv()

    def g_start(a, *ks):
        for k in ks:
            g_copy(a, k).start()

    def compact(a):
        x_wait(a)
        full[a, x, :, part_of(c)] = dot(pick_m[...], in_x[a]).astype(BF16)
        g_start(a, 1, 2, 0)

    def gate_up(xx, first):
        def body(n, carry):
            cols = pl.ds(pl.multiple_of(n * WIDE, WIDE), WIDE)
            for acc, w in ((gate_acc, gate_v), (up_acc, up_v)):
                term = dot(full[0, xx], w[xx, :, cols])
                acc[:, cols] = term if first else acc[:, cols] + term
            return carry

        lax.fori_loop(0, HID // WIDE, body, 0)

    def flip_rows(xx):
        rows_t[xx] = full[0, xx].T
        pltpu.make_async_copy(rows_t.at[xx], rows_t_hbm.at[xx], o_sem.at[0, xx]).start()

    def back(xx, first):
        def body(n, carry):
            cols = pl.ds(pl.multiple_of(n * WIDE, WIDE), WIDE)
            term = dot_t(full[1, xx], down_v[xx, cols, :])
            back_acc[:, cols] = term if first else back_acc[:, cols] + term
            return carry

        lax.fori_loop(0, HID // WIDE, body, 0)

    compact(0)
    for copy in weight_copies[:2]:
        copy.wait()
    compact(1)
    g_wait(0, 0)
    gate_up(x, True)
    g_wait(0, 1)
    g_start(0, 5, 3)
    g_wait(0, 2)
    g_start(0, 6, 4)
    flip_rows(x)
    g_wait(0, 3)
    gate_up(left, False)
    g_wait(0, 4)
    gate_up(right, False)
    g_wait(0, 5, 6)
    g_start(0, 7, 8)
    for copy in weight_copies[2:]:
        copy.wait()
    g_wait(1, 0)
    back(x, True)
    g_wait(1, 1)
    g_start(1, 5, 3)
    g_wait(1, 2)
    g_start(1, 6, 4)
    g_wait(0, 7, 8)
    gate_up(opp, False)

    def activate(i, carry):
        rows = pl.ds(pl.multiple_of(i * 16, 16), 16)
        pre, up = gate_acc[rows, :], up_acc[rows, :]
        sigma = jax.nn.sigmoid(pre)
        silu = pre * sigma
        hidden[rows, :] = (silu * up).astype(BF16)
        gate_acc[rows, :] = up * sigma * (1.0 + pre * (1.0 - sigma))
        up_acc[rows, :] = silu
        return carry

    lax.fori_loop(0, CAP // 16, activate, 0)
    flip_rows(left)
    g_wait(1, 3)
    back(left, False)
    g_wait(1, 4)
    back(right, False)
    flip_rows(right)
    g_wait(1, 5, 6)
    g_start(1, 7, 8)
    flip_rows(opp)
    hidden_t[...] = hidden[...].T
    hidden_copy = pltpu.make_async_copy(hidden_t, hidden_t_hbm, o_sem.at[2, 0])
    hidden_copy.start()

    g_wait(1, 7, 8)
    back(opp, False)

    def finish(i, carry):
        rows = pl.ds(pl.multiple_of(i * 16, 16), 16)
        bh = back_acc[rows, :]
        gain = gain_col[rows, 0:1]
        dh = gain * bh
        ggp[rows, :] = (dh * gate_acc[rows, :]).astype(BF16)
        gup[rows, :] = (dh * up_acc[rows, :]).astype(BF16)
        prod = hidden[rows, :].astype(F32) * bh
        part = prod[:, 0:128]
        for j in range(1, HID // 128):
            part = part + prod[:, j * 128 : (j + 1) * 128]
        back_acc[rows, 0:128] = part
        return carry

    lax.fori_loop(0, CAP // 16, finish, 0)
    grad_copies = [
        pltpu.make_async_copy(ggp, ggp_hbm, o_sem.at[2, 1]),
        pltpu.make_async_copy(gup, gup_hbm, o_sem.at[2, 2]),
    ]
    for copy in grad_copies:
        copy.start()

    def contrib(xx, cc):
        feats = part_of(cc)
        return dot_t(ggp[...], gate_v[xx, feats, :]) + dot_t(gup[...], up_v[xx, feats, :])

    def s_copy(k, xx):
        return pltpu.make_async_remote_copy(
            src_ref=sib_out.at[xx], dst_ref=sib_in.at[xx], send_sem=s_send.at[k], recv_sem=s_recv.at[k],
            device_id=(seq, x * 2 + oc), device_id_type=MESH,
        )

    def r_copy(k):
        src, dst, target = (
            (rel_out.at[0], rel_in.at[0], right),
            (rel_out.at[1], rel_in.at[1], left),
            (dir_out.at[0], dir_in.at[0], right),
            (dir_out.at[1], dir_in.at[1], left),
            (fin_out.at[0], fin_in.at[0], right),
            (fin_out.at[1], fin_in.at[1], left),
        )[k]
        return pltpu.make_async_remote_copy(
            src_ref=src, dst_ref=dst, send_sem=r_send.at[k], recv_sem=r_recv.at[k],
            device_id=(seq, target * 2 + c), device_id_type=MESH,
        )

    order = (opp, right, left, x)

    def for_sibling(k):
        sib_out[order[k]] = contrib(order[k], oc).astype(BF16)
        s_copy(k, order[k]).start()

    def for_chip(k):
        sums[k] = contrib(order[k], c)

    def add_sibling(k):
        s_copy(k, order[k]).wait_recv()
        sums[k] = sums[k] + sib_in[order[k]].astype(F32)

    for_sibling(0)
    for_sibling(1)
    for_chip(0)
    add_sibling(0)
    rel_out[0] = sums[0, 0:HALF, :].astype(BF16)
    rel_out[1] = sums[0, HALF:CAP, :].astype(BF16)
    r_copy(0).start()
    r_copy(1).start()
    for_sibling(2)
    for_chip(1)
    add_sibling(1)
    dir_out[0] = sums[1, HALF:CAP, :].astype(BF16)
    r_copy(2).start()
    for_chip(2)
    add_sibling(2)
    dir_out[1] = sums[2, 0:HALF, :].astype(BF16)
    r_copy(3).start()
    for_sibling(3)

    score_part = jnp.sum(back_acc[:, 0:128].T, axis=0, keepdims=True)
    score_buf[ex] = jnp.broadcast_to(score_part, (8, CAP))

    def q_copy(peer, slot):
        return pltpu.make_async_remote_copy(
            src_ref=score_buf.at[ex], dst_ref=score_buf.at[slot], send_sem=q_send.at[peer], recv_sem=q_recv.at[slot],
            device_id=(seq, peer), device_id_type=MESH,
        )

    def q_start(k, carry):
        q_copy(lax.rem(ex + k, 8), ex).start()
        return carry

    r_copy(0).wait_recv()
    fin_out[0] = (sums[1, 0:HALF, :] + rel_in[0].astype(F32)).astype(BF16)
    r_copy(4).start()
    r_copy(1).wait_recv()
    fin_out[1] = (sums[2, HALF:CAP, :] + rel_in[1].astype(F32)).astype(BF16)
    r_copy(5).start()
    lax.fori_loop(1, 8, q_start, 0)
    for_chip(3)
    add_sibling(3)

    for k in range(9):
        g_copy(1, k).wait_send()
    for i in range(CHIPS):
        gain = gain_col[:, 0:1]
        full[1, i] = (gain * full[1, i].astype(F32)).astype(BF16)
        pltpu.make_async_copy(full.at[1, i], scaled_hbm.at[i], o_sem.at[1, i]).start()

    for k in (2, 3, 4, 5):
        r_copy(k).wait_recv()
    low = sums[3, 0:HALF, :] + fin_in[0].astype(F32) + dir_in[1].astype(F32)
    high = sums[3, HALF:CAP, :] + dir_in[0].astype(F32) + fin_in[1].astype(F32)
    summed = jnp.concatenate([low.astype(BF16), high.astype(BF16)], axis=0)
    out_r[...] = dot(pick_t[...], summed).astype(BF16)

    def c_copy(peer, slot):
        return pltpu.make_async_remote_copy(
            src_ref=out_r.at[pl.ds(pl.multiple_of(peer * MOST, MOST), MOST), :],
            dst_ref=in_r.at[pl.ds(pl.multiple_of(slot * MOST, MOST), MOST), :],
            send_sem=c_send.at[peer],
            recv_sem=c_recv.at[slot],
            device_id=(peer, ex),
            device_id_type=MESH,
        )

    def c_start(k, carry):
        c_copy(seq_peer(k), seq).start()
        return carry

    def c_wait(k, carry):
        peer = seq_peer(k)
        c_copy(peer, peer).wait_recv()
        return carry

    lax.fori_loop(1, OWNERS, c_start, 0)
    here = pl.ds(pl.multiple_of(seq * MOST, MOST), MOST)
    in_r[here, :] = out_r[here, :]

    for g in range(OWNERS // 2):
        here = slice(g * 2 * MOST, (g + 1) * 2 * MOST)
        send_t[:, here] = send_m[here, :].astype(F32).T.astype(BF16)

    def q_wait(k, carry):
        peer = lax.rem(ex + k, 8)
        q_copy(peer, peer).wait_recv()
        return carry

    lax.fori_loop(1, 8, q_wait, 0)
    total = score_buf[0, 0:1, :]
    for i in range(1, 8):
        total = total + score_buf[i, 0:1, :]
    score_out[...] = total

    lax.fori_loop(1, OWNERS, c_wait, 0)
    tok_out[...] = dot(send_t[...], in_r[...]).astype(BF16)

    def sent(k, carry):
        peer = seq_peer(k)
        x_copy(0, peer, seq).wait_send()
        x_copy(1, peer, seq).wait_send()
        c_copy(peer, seq).wait_send()
        return carry

    def q_sent(k, carry):
        q_copy(lax.rem(ex + k, 8), ex).wait_send()
        return carry

    lax.fori_loop(1, OWNERS, sent, 0)
    lax.fori_loop(1, 8, q_sent, 0)
    for k in range(9):
        g_copy(0, k).wait_send()
    for k in range(4):
        s_copy(k, order[k]).wait_send()
    for k in range(6):
        r_copy(k).wait_send()
    for i in range(CHIPS):
        pltpu.make_async_copy(rows_t.at[i], rows_t_hbm.at[i], o_sem.at[0, i]).wait()
        pltpu.make_async_copy(full.at[1, i], scaled_hbm.at[i], o_sem.at[1, i]).wait()
    hidden_copy.wait()
    for copy in grad_copies:
        copy.wait()


def weight_kernel(rows_t, scaled, hidden_t, ggp, gup, grad_gate, grad_up, grad_down):
    grad_gate[...] = dot(rows_t[...], ggp[...]).astype(BF16)
    grad_up[...] = dot(rows_t[...], gup[...]).astype(BF16)
    grad_down[...] = dot(hidden_t[...], scaled[...]).astype(BF16)


def shards(tokens, grad_out, chosen, scores, gate_weight, up_weight, down_weight):
    vmem = pl.BlockSpec(memory_space=pltpu.VMEM)
    anyw = pl.BlockSpec(memory_space=pl.ANY)
    shape = jax.ShapeDtypeStruct
    dma = pltpu.SemaphoreType.DMA
    tok, score, rows_t, scaled, hidden_t, ggp, gup = pl.pallas_call(
        layer_kernel,
        out_shape=(
            shape((CAP, PART), BF16),
            shape((1, CAP), F32),
            shape((CHIPS, WIDE, CAP), BF16),
            shape((CHIPS, CAP, WIDE), BF16),
            shape((HID, CAP), BF16),
            shape((CAP, HID), BF16),
            shape((CAP, HID), BF16),
        ),
        in_specs=[vmem] * 4 + [anyw] * 3,
        out_specs=(vmem, vmem) + (anyw,) * 5,
        scratch_shapes=[
            pltpu.VMEM((CHIPS, WIDE, HID), BF16),
            pltpu.VMEM((CHIPS, WIDE, HID), BF16),
            pltpu.VMEM((CHIPS, HID, WIDE), BF16),
            pltpu.VMEM((2, CHIPS, CAP, WIDE), BF16),
            pltpu.VMEM((CAP, HID), F32),
            pltpu.VMEM((CAP, HID), F32),
            pltpu.VMEM((CAP, HID), F32),
            pltpu.VMEM((CAP, HID), BF16),
            pltpu.VMEM((HID, CAP), BF16),
            pltpu.VMEM((CAP, HID), BF16),
            pltpu.VMEM((CAP, HID), BF16),
            pltpu.VMEM((CHIPS, WIDE, CAP), BF16),
            pltpu.VMEM((OWNERS * MOST, CAP), BF16),
            pltpu.VMEM((CAP, OWNERS * MOST), BF16),
            pltpu.VMEM((CAP, OWNERS * MOST), BF16),
            pltpu.VMEM((OWNERS * MOST, CAP), BF16),
            pltpu.VMEM((2, OWNERS * MOST, PART), BF16),
            pltpu.VMEM((2, OWNERS * MOST, PART), BF16),
            pltpu.VMEM((OWNERS * MOST, PART), BF16),
            pltpu.VMEM((OWNERS * MOST, PART), BF16),
            pltpu.VMEM((CHIPS, CAP, PART), F32),
            pltpu.VMEM((CHIPS, CAP, PART), BF16),
            pltpu.VMEM((CHIPS, CAP, PART), BF16),
        ]
        + [pltpu.VMEM((2, HALF, PART), BF16)] * 6
        + [
            pltpu.VMEM((8, 8, CAP), F32),
            pltpu.VMEM((CAP, 128), F32),
            dma((2 + CHIPS,)),
            dma((3, CHIPS)),
            dma((2, OWNERS)),
            dma((2, OWNERS)),
            dma((2, 9)),
            dma((2, 9)),
            dma((4,)),
            dma((4,)),
            dma((OWNERS,)),
            dma((OWNERS,)),
            dma((6,)),
            dma((6,)),
            dma((8,)),
            dma((8,)),
        ],
        compiler_params=pltpu.CompilerParams(
            collective_id=0, has_side_effects=True, vmem_limit_bytes=VMEM_BYTES
        ),
        name="layer",
    )(
        tokens,
        grad_out,
        chosen,
        scores,
        gate_weight.reshape(CHIPS, WIDE, HID),
        up_weight.reshape(CHIPS, WIDE, HID),
        down_weight,
    )
    whole = lambda i: (0, 0)
    none = pl.squeezed
    grad_gate, grad_up, grad_down = pl.pallas_call(
        weight_kernel,
        grid=(CHIPS,),
        out_shape=(
            shape((1, CHIPS * WIDE, HID), BF16),
            shape((1, CHIPS * WIDE, HID), BF16),
            shape((1, HID, CHIPS * WIDE), BF16),
        ),
        in_specs=[
            pl.BlockSpec((none, WIDE, CAP), lambda i: (i, 0, 0)),
            pl.BlockSpec((none, CAP, WIDE), lambda i: (i, 0, 0)),
            pl.BlockSpec((HID, CAP), whole),
            pl.BlockSpec((CAP, HID), whole),
            pl.BlockSpec((CAP, HID), whole),
        ],
        out_specs=(
            pl.BlockSpec((none, WIDE, HID), lambda i: (0, i, 0)),
            pl.BlockSpec((none, WIDE, HID), lambda i: (0, i, 0)),
            pl.BlockSpec((none, HID, WIDE), lambda i: (0, 0, i)),
        ),
        compiler_params=pltpu.CompilerParams(vmem_limit_bytes=VMEM_BYTES),
        name="weight_grads",
    )(rows_t, scaled, hidden_t, ggp, gup)
    return tok, score, grad_gate, grad_up, grad_down


def solution(mesh):
    in_specs = (
        P("seq", "exp"),
        P("seq", "exp"),
        P(),
        P("seq", None),
        P("seq", None, "exp"),
        P("seq", None, "exp"),
        P("seq", "exp", None),
    )
    out_specs = (
        P("seq", "exp"),
        P("seq", None),
        P("seq", None, "exp"),
        P("seq", None, "exp"),
        P("seq", "exp", None),
    )
    return jax.shard_map(shards, mesh=mesh, in_specs=in_specs, out_specs=out_specs, check_vma=False)
```

```python
import functools

import jax
import jax.numpy as jnp
from jax import lax
from jax.experimental import pallas as pl
from jax.experimental.pallas import tpu as pltpu
from jax.sharding import PartitionSpec as P

MESH = pl.DeviceIdType.MESH
BF16 = jnp.bfloat16
F32 = jnp.float32

OWNERS = 16
MOST = 64
CAP = 512
PART = 256
CHIPS = 4
WIDE = 512
HID = 1024
LANES = 128
VMEM_BYTES = 50 * 1024 * 1024


def dot(a, b):
    return jnp.dot(a, b, preferred_element_type=F32)


def dot_t(a, b):
    return lax.dot_general(a, b, (((1,), (1,)), ((), ())), preferred_element_type=F32)


def iota(shape, axis):
    return lax.broadcasted_iota(jnp.int32, shape, axis)


def part_of(c):
    return pl.ds(pl.multiple_of(c * PART, PART), PART)


def layer_kernel(
    tokens, grads_in, chosen, scores, gate_hbm, up_hbm, down_hbm,
    tok_out, score_out, grad_gate, grad_up, grad_down,
    gate_v, up_v, down_v, full, gate_acc, up_acc, back_acc, hidden, hidden_t, ggp, gup,
    rows_t, send_m, send_t, pick_m, pick_t, out_x, in_x, out_r, in_r, sib_out, sib_in,
    rel_out, rel_in, dir_out, dir_in, fin_out, fin_in, score_buf, gain_col,
    w_sem, x_send, x_recv, g_send, g_recv, s_send, s_recv, c_send, c_recv, r_send, r_recv,
    q_send, q_recv,
):
    seq = lax.axis_index("seq")
    ex = lax.axis_index("exp")
    zz, yy = seq // 4, lax.rem(seq, 4)
    x, c = ex // 2, lax.rem(ex, 2)
    right, left, opp = lax.rem(x + 1, 4), lax.rem(x + 3, 4), lax.rem(x + 2, 4)
    oc = 1 - c

    def seq_peer(k):
        dz, dy = k // 4, lax.rem(k, 4)
        return lax.rem(zz + dz, 4) * 4 + lax.rem(yy + dy, 4)

    def each_peer(step):
        def body(k, carry):
            step(seq_peer(k))
            return carry

        lax.fori_loop(1, OWNERS, body, 0)

    def each_part(step):
        def body(k, carry):
            step(lax.rem(ex + k, 8))
            return carry

        lax.fori_loop(1, 8, body, 0)

    weight_copies = [
        pltpu.make_async_copy(gate_hbm, gate_v, w_sem.at[0]),
        pltpu.make_async_copy(up_hbm, up_v, w_sem.at[1]),
    ] + [
        pltpu.make_async_copy(down_hbm.at[0, :, pl.ds(i * WIDE, WIDE)], down_v.at[i], w_sem.at[2 + i])
        for i in range(CHIPS)
    ]

    barrier = pltpu.get_barrier_semaphore()

    def greet(s, e):
        pl.semaphore_signal(barrier, inc=1, device_id=(s, e), device_id_type=MESH)

    each_peer(lambda peer: greet(peer, ex))
    each_part(lambda peer: greet(seq, peer))
    for copy in weight_copies:
        copy.start()

    lower = seq * CAP
    table = chosen[...]
    begins = jnp.sum((table < lower).astype(jnp.int32), axis=1, keepdims=True)
    mine = jnp.logical_and(table >= lower, table < lower + CAP)
    slots = jnp.where(mine, iota((OWNERS, CAP), 1) - begins, -1)
    local = table - lower
    sub = iota((MOST, CAP), 0)
    lanes = iota((MOST, CAP), 1)
    for e in range(OWNERS):
        hit = slots[e : e + 1, :] == sub
        token = jnp.sum(jnp.where(hit, local[e : e + 1, :] + 1, 0), axis=1, keepdims=True) - 1
        send_m[e * MOST : (e + 1) * MOST, :] = jnp.where(token == lanes, 1.0, 0.0).astype(BF16)

    def slot(owner):
        return pl.ds(pl.multiple_of(owner * MOST, MOST), MOST)

    def x_copy(ch, peer, place):
        return pltpu.make_async_remote_copy(
            src_ref=out_x.at[ch, slot(peer), :],
            dst_ref=in_x.at[ch, slot(place), :],
            send_sem=x_send.at[ch, peer],
            recv_sem=x_recv.at[ch, place],
            device_id=(peer, ex),
            device_id_type=MESH,
        )

    def pack(a, source):
        block = dot(send_m[...], source[...]).astype(BF16)
        out_x[2 * a] = block[:, 0:LANES]
        out_x[2 * a + 1] = block[:, LANES:PART]

    def x_start(ch):
        each_peer(lambda peer: x_copy(ch, peer, seq).start())
        in_x[ch, slot(seq), :] = out_x[ch, slot(seq), :]

    pack(0, tokens)
    pl.semaphore_wait(barrier, OWNERS - 1 + 7)
    x_start(0)
    x_start(1)
    pack(1, grads_in)
    x_start(2)
    x_start(3)

    picked = chosen[pl.ds(seq, 1), :]
    owner_low = iota((OWNERS, CAP), 0) * CAP
    wide = jnp.broadcast_to(picked, (OWNERS, CAP))
    firsts = jnp.sum((wide < owner_low).astype(jnp.int32), axis=1, keepdims=True)
    inside = jnp.logical_and(wide >= owner_low, wide < owner_low + CAP)
    places = jnp.where(inside, iota((OWNERS, CAP), 1) - firsts, -1)
    for g in range(OWNERS // 2):
        block = jnp.concatenate(
            [jnp.where(places[o : o + 1, :] == sub, 1.0, 0.0) for o in (2 * g, 2 * g + 1)], axis=0
        )
        here = slice(g * 2 * MOST, (g + 1) * 2 * MOST)
        pick_t[here, :] = block.astype(BF16)
        pick_m[:, here] = block.T.astype(BF16)
    gain_col[...] = jnp.broadcast_to(scores[...], (128, CAP)).T

    def region(ch, xx, cc):
        a, f = ch // 2, ch % 2
        return full.at[a, xx, :, pl.ds(pl.multiple_of(cc * PART + f * LANES, LANES), LANES)]

    def g_copy(ch, k):
        f = ch % 2
        view, target = {
            0: (region(ch, x, c), (x, oc)),
            1: (region(ch, x, c), (right, c)),
            2: (region(ch, x, c), (left, c)),
            3: (region(ch, left, c), (x, oc)),
            4: (region(ch, right, c), (x, oc)),
            5: (region(ch, left, c), (right, c)) if f == 0 else (region(ch, right, c), (left, c)),
            6: (region(ch, opp, c), (x, oc)),
        }[k]
        return pltpu.make_async_remote_copy(
            src_ref=view, dst_ref=view, send_sem=g_send.at[ch, k], recv_sem=g_recv.at[ch, k],
            device_id=(seq, target[0] * 2 + target[1]), device_id_type=MESH,
        )

    def g_wait(ch, k):
        g_copy(ch, k).wait_recv()

    def g_start(ch, k):
        g_copy(ch, k).start()

    def compact(ch):
        each_peer(lambda peer: x_copy(ch, peer, peer).wait_recv())
        a, f = ch // 2, ch % 2
        cols = pl.ds(pl.multiple_of(c * PART + f * LANES, LANES), LANES)
        full[a, x, :, cols] = dot(pick_m[...], in_x[ch]).astype(BF16)
        for k in (1, 2, 0) if f == 0 else (2, 1, 0):
            g_start(ch, k)

    def relay(ch):
        for k in (1, 2) if ch % 2 == 0 else (2, 1):
            g_wait(ch, k)
            if k == 1 + ch % 2:
                g_start(ch, 5)
            g_start(ch, 2 + k)

    def relay_opp(ch):
        g_wait(ch, 5)
        g_start(ch, 6)

    def gate_up(xx, first):
        def body(n, carry):
            cols = pl.ds(pl.multiple_of(n * WIDE, WIDE), WIDE)
            for acc, w in ((gate_acc, gate_v), (up_acc, up_v)):
                term = dot(full[0, xx], w[xx, :, cols])
                acc[:, cols] = term if first else acc[:, cols] + term
            return carry

        lax.fori_loop(0, HID // WIDE, body, 0)

    def flip_rows(xx):
        rows_t[xx] = full[0, xx].T

    def back(xx, first):
        def body(n, carry):
            cols = pl.ds(pl.multiple_of(n * WIDE, WIDE), WIDE)
            term = dot_t(full[1, xx], down_v[xx, cols, :])
            back_acc[:, cols] = term if first else back_acc[:, cols] + term
            return carry

        lax.fori_loop(0, HID // WIDE, body, 0)

    compact(0)
    compact(1)
    relay(0)
    compact(2)
    relay(1)
    compact(3)
    for copy in weight_copies:
        copy.wait()
    g_wait(0, 0)
    g_wait(1, 0)
    gate_up(x, True)
    relay(2)
    relay_opp(0)
    relay_opp(1)
    g_wait(0, 3)
    g_wait(1, 3)
    gate_up(left, False)
    relay(3)
    g_wait(0, 4)
    g_wait(1, 4)
    gate_up(right, False)
    g_wait(0, 6)
    g_wait(1, 6)
    gate_up(opp, False)
    relay_opp(2)

    def activate(i, carry):
        rows = pl.ds(pl.multiple_of(i * 16, 16), 16)
        pre, up = gate_acc[rows, :], up_acc[rows, :]
        gain = gain_col[rows, 0:1]
        sigma = jax.nn.sigmoid(pre)
        silu = pre * sigma
        hidden[rows, :] = (silu * up).astype(BF16)
        gate_acc[rows, :] = gain * up * sigma * (1.0 + pre * (1.0 - sigma))
        up_acc[rows, :] = gain * silu
        return carry

    lax.fori_loop(0, CAP // 16, activate, 0)
    g_wait(2, 0)
    g_wait(3, 0)
    back(x, True)
    g_wait(2, 3)
    g_wait(3, 3)
    back(left, False)
    g_wait(2, 4)
    g_wait(3, 4)
    back(right, False)
    relay_opp(3)
    flip_rows(x)
    flip_rows(left)
    g_wait(2, 6)
    g_wait(3, 6)
    back(opp, False)

    def finish(i, carry):
        rows = pl.ds(pl.multiple_of(i * 16, 16), 16)
        bh = back_acc[rows, :]
        ggp[rows, :] = (bh * gate_acc[rows, :]).astype(BF16)
        gup[rows, :] = (bh * up_acc[rows, :]).astype(BF16)
        return carry

    lax.fori_loop(0, CAP // 16, finish, 0)

    def contrib(xx, cc):
        feats = part_of(cc)
        return dot_t(ggp[...], gate_v[xx, feats, :]) + dot_t(gup[...], up_v[xx, feats, :])

    order = (opp, left, right, x)

    def s_copy(k):
        return pltpu.make_async_remote_copy(
            src_ref=sib_out.at[k], dst_ref=sib_in.at[k], send_sem=s_send.at[k], recv_sem=s_recv.at[k],
            device_id=(seq, x * 2 + oc), device_id_type=MESH,
        )

    def r_copy(k):
        src, dst, target = (
            (rel_out.at[0], rel_in.at[0], right),
            (rel_out.at[1], rel_in.at[1], left),
            (dir_out.at[0], dir_in.at[0], left),
            (dir_out.at[1], dir_in.at[1], right),
            (fin_out.at[0], fin_in.at[0], right),
            (fin_out.at[1], fin_in.at[1], left),
        )[k]
        return pltpu.make_async_remote_copy(
            src_ref=src, dst_ref=dst, send_sem=r_send.at[k], recv_sem=r_recv.at[k],
            device_id=(seq, target * 2 + c), device_id_type=MESH,
        )

    def for_sibling(k):
        sib_out[k] = contrib(order[k], oc).astype(BF16)
        s_copy(k).start()

    def sums(k, f):
        return gate_acc[:, k * PART + f * LANES : k * PART + (f + 1) * LANES]

    def for_chip(k):
        gate_acc[:, k * PART : (k + 1) * PART] = contrib(order[k], c)

    def add_sibling(k):
        s_copy(k).wait_recv()
        here = slice(k * PART, (k + 1) * PART)
        gate_acc[:, here] = gate_acc[:, here] + sib_in[k].astype(F32)

    for_sibling(0)
    for_sibling(1)
    for_chip(0)
    add_sibling(0)
    rel_out[0] = sums(0, 0).astype(BF16)
    r_copy(0).start()
    rel_out[1] = sums(0, 1).astype(BF16)
    r_copy(1).start()
    for_sibling(2)
    for_chip(1)
    add_sibling(1)
    dir_out[0] = sums(1, 0).astype(BF16)
    r_copy(2).start()
    for_chip(2)
    add_sibling(2)
    dir_out[1] = sums(2, 1).astype(BF16)
    r_copy(3).start()
    for_sibling(3)

    def score_rows(i, carry):
        rows = pl.ds(pl.multiple_of(i * 16, 16), 16)
        prod = hidden[rows, :].astype(F32) * back_acc[rows, :]
        part = prod[:, 0:128]
        for j in range(1, HID // 128):
            part = part + prod[:, j * 128 : (j + 1) * 128]
        back_acc[rows, 0:128] = part
        return carry

    def q_copy(peer, place):
        return pltpu.make_async_remote_copy(
            src_ref=score_buf.at[ex], dst_ref=score_buf.at[place], send_sem=q_send.at[peer], recv_sem=q_recv.at[place],
            device_id=(seq, peer), device_id_type=MESH,
        )

    lax.fori_loop(0, CAP // 16, score_rows, 0)
    r_copy(0).wait_recv()
    fin_out[0] = (sums(2, 0) + rel_in[0].astype(F32)).astype(BF16)
    r_copy(4).start()
    r_copy(1).wait_recv()
    fin_out[1] = (sums(1, 1) + rel_in[1].astype(F32)).astype(BF16)
    r_copy(5).start()
    for_chip(3)
    score_part = jnp.sum(back_acc[:, 0:128].T, axis=0, keepdims=True)
    score_buf[ex] = jnp.broadcast_to(score_part, (8, CAP))
    each_part(lambda peer: q_copy(peer, ex).start())

    def weight_rows(xx):
        def body(n, carry):
            cols = pl.ds(pl.multiple_of(n * WIDE, WIDE), WIDE)
            here = pl.ds(pl.multiple_of(xx * WIDE, WIDE), WIDE)
            grad_gate[here, cols] = dot(rows_t[xx], ggp[:, cols]).astype(BF16)
            grad_up[here, cols] = dot(rows_t[xx], gup[:, cols]).astype(BF16)
            return carry

        lax.fori_loop(0, HID // WIDE, body, 0)

    def weight_down(i):
        full[1, i] = (gain_col[:, 0:1] * full[1, i].astype(F32)).astype(BF16)

        def body(n, carry):
            here = pl.ds(pl.multiple_of(n * WIDE, WIDE), WIDE)
            grad_down[here, i * WIDE : (i + 1) * WIDE] = dot(hidden_t[here, :], full[1, i]).astype(BF16)
            return carry

        lax.fori_loop(0, HID // WIDE, body, 0)

    def c_copy(f, peer, place):
        return pltpu.make_async_remote_copy(
            src_ref=out_r.at[f, slot(peer), :],
            dst_ref=in_r.at[f, slot(place), :],
            send_sem=c_send.at[f, peer],
            recv_sem=c_recv.at[f, place],
            device_id=(peer, ex),
            device_id_type=MESH,
        )

    def give_back(f):
        r_copy(2 + f).wait_recv()
        r_copy(4 + f).wait_recv()
        summed = (sums(3, f) + fin_in[f].astype(F32) + dir_in[f].astype(F32)).astype(BF16)
        out_r[f] = dot(pick_t[...], summed).astype(BF16)
        each_peer(lambda peer: c_copy(f, peer, seq).start())
        in_r[f, slot(seq), :] = out_r[f, slot(seq), :]

    weight_rows(x)
    add_sibling(3)
    weight_rows(left)
    flip_rows(right)
    give_back(0)
    weight_rows(right)
    give_back(1)
    flip_rows(opp)
    weight_rows(opp)
    hidden_t[...] = hidden[...].T
    for ch in (2, 3):
        for k in range(7):
            g_copy(ch, k).wait_send()
    for i in range(CHIPS):
        weight_down(i)
    for g in range(OWNERS // 2):
        here = slice(g * 2 * MOST, (g + 1) * 2 * MOST)
        send_t[:, here] = send_m[here, :].astype(F32).T.astype(BF16)

    each_part(lambda peer: q_copy(peer, peer).wait_recv())
    total = score_buf[0, 0:1, :]
    for i in range(1, 8):
        total = total + score_buf[i, 0:1, :]
    score_out[...] = total

    for f in range(2):
        each_peer(lambda peer: c_copy(f, peer, peer).wait_recv())
        tok_out[:, f * LANES : (f + 1) * LANES] = dot(send_t[...], in_r[f]).astype(BF16)

    def sent(peer):
        for ch in range(4):
            x_copy(ch, peer, seq).wait_send()
        for f in range(2):
            c_copy(f, peer, seq).wait_send()

    each_peer(sent)
    each_part(lambda peer: q_copy(peer, ex).wait_send())
    for k in range(7):
        g_copy(0, k).wait_send()
        g_copy(1, k).wait_send()
    for k in range(4):
        s_copy(k).wait_send()
    for k in range(6):
        r_copy(k).wait_send()


def store_kernel(*refs):
    count = (len(refs) - 1) // 2
    sems = refs[-1]
    copies = []
    for src, dst in zip(refs[:count], refs[count : 2 * count]):
        cuts = 4 if src.shape[0] >= 1024 else 1
        rows = src.shape[0] // cuts
        for i in range(cuts):
            here = pl.ds(i * rows, rows)
            copies.append(pltpu.make_async_copy(src.at[here, :], dst.at[here, :], sems.at[len(copies)]))
    for copy in copies:
        copy.start()
    for copy in copies:
        copy.wait()


def shards(tokens, grad_out, chosen, scores, gate_weight, up_weight, down_weight):
    vmem = pl.BlockSpec(memory_space=pltpu.VMEM)
    anyw = pl.BlockSpec(memory_space=pl.ANY)
    shape = jax.ShapeDtypeStruct
    dma = pltpu.SemaphoreType.DMA
    results = (
        ((CAP, PART), BF16),
        ((1, CAP), F32),
        ((CHIPS * WIDE, HID), BF16),
        ((CHIPS * WIDE, HID), BF16),
        ((HID, CHIPS * WIDE), BF16),
    )
    kept = pl.pallas_call(
        layer_kernel,
        out_shape=tuple(pltpu.VMEM(*r) for r in results),
        in_specs=[vmem] * 4 + [anyw] * 3,
        out_specs=(vmem,) * 5,
        scratch_shapes=[
            pltpu.VMEM((CHIPS, WIDE, HID), BF16),
            pltpu.VMEM((CHIPS, WIDE, HID), BF16),
            pltpu.VMEM((CHIPS, HID, WIDE), BF16),
            pltpu.VMEM((2, CHIPS, CAP, WIDE), BF16),
            pltpu.VMEM((CAP, HID), F32),
            pltpu.VMEM((CAP, HID), F32),
            pltpu.VMEM((CAP, HID), F32),
            pltpu.VMEM((CAP, HID), BF16),
            pltpu.VMEM((HID, CAP), BF16),
            pltpu.VMEM((CAP, HID), BF16),
            pltpu.VMEM((CAP, HID), BF16),
            pltpu.VMEM((CHIPS, WIDE, CAP), BF16),
            pltpu.VMEM((OWNERS * MOST, CAP), BF16),
            pltpu.VMEM((CAP, OWNERS * MOST), BF16),
            pltpu.VMEM((CAP, OWNERS * MOST), BF16),
            pltpu.VMEM((OWNERS * MOST, CAP), BF16),
            pltpu.VMEM((4, OWNERS * MOST, LANES), BF16),
            pltpu.VMEM((4, OWNERS * MOST, LANES), BF16),
            pltpu.VMEM((2, OWNERS * MOST, LANES), BF16),
            pltpu.VMEM((2, OWNERS * MOST, LANES), BF16),
            pltpu.VMEM((CHIPS, CAP, PART), BF16),
            pltpu.VMEM((CHIPS, CAP, PART), BF16),
        ]
        + [pltpu.VMEM((2, CAP, LANES), BF16)] * 6
        + [
            pltpu.VMEM((8, 8, CAP), F32),
            pltpu.VMEM((CAP, 128), F32),
            dma((2 + CHIPS,)),
            dma((4, OWNERS)),
            dma((4, OWNERS)),
            dma((4, 7)),
            dma((4, 7)),
            dma((4,)),
            dma((4,)),
            dma((2, OWNERS)),
            dma((2, OWNERS)),
            dma((6,)),
            dma((6,)),
            dma((8,)),
            dma((8,)),
        ],
        compiler_params=pltpu.CompilerParams(
            collective_id=0, has_side_effects=True, vmem_limit_bytes=VMEM_BYTES
        ),
        name="layer",
    )(
        tokens,
        grad_out,
        chosen,
        scores,
        gate_weight.reshape(CHIPS, WIDE, HID),
        up_weight.reshape(CHIPS, WIDE, HID),
        down_weight,
    )
    tok, score, grad_gate, grad_up, grad_down = pl.pallas_call(
        store_kernel,
        out_shape=tuple(shape(*r) for r in results),
        in_specs=[vmem] * 5,
        out_specs=(anyw,) * 5,
        scratch_shapes=[dma((16,))],
        compiler_params=pltpu.CompilerParams(vmem_limit_bytes=1024 * 1024),
        name="store",
    )(*[pltpu.with_memory_space_constraint(k, pltpu.VMEM) for k in kept])
    return tok, score, grad_gate[None], grad_up[None], grad_down[None]


def solution(mesh):
    in_specs = (
        P("seq", "exp"),
        P("seq", "exp"),
        P(),
        P("seq", None),
        P("seq", None, "exp"),
        P("seq", None, "exp"),
        P("seq", "exp", None),
    )
    out_specs = (
        P("seq", "exp"),
        P("seq", None),
        P("seq", None, "exp"),
        P("seq", None, "exp"),
        P("seq", "exp", None),
    )
    return jax.shard_map(shards, mesh=mesh, in_specs=in_specs, out_specs=out_specs, check_vma=False)
```

```python
import functools

import jax
import jax.numpy as jnp
from jax import lax
from jax.experimental import pallas as pl
from jax.experimental.pallas import tpu as pltpu
from jax.sharding import PartitionSpec as P

MESH = pl.DeviceIdType.MESH
BF16 = jnp.bfloat16
F32 = jnp.float32

OWNERS = 16
MOST = 64
CAP = 512
PART = 256
CHIPS = 4
WIDE = 512
HID = 1024
LANES = 128
HALF = CAP // 2
VMEM_BYTES = 50 * 1024 * 1024


def dot(a, b):
    return jnp.dot(a, b, preferred_element_type=F32)


def dot_t(a, b):
    return lax.dot_general(a, b, (((1,), (1,)), ((), ())), preferred_element_type=F32)


def iota(shape, axis):
    return lax.broadcasted_iota(jnp.int32, shape, axis)


def part_of(c):
    return pl.ds(pl.multiple_of(c * PART, PART), PART)


def layer_kernel(
    tokens, grads_in, chosen, scores, gate_hbm, up_hbm, down_hbm,
    tok_out, score_out, grad_gate, grad_up, hidden_t, scaled,
    gate_v, up_v, down_v, full, gate_acc, up_acc, back_acc, hidden, ggp, gup,
    rows_t, send_m, send_t, pick_m, pick_t, out_x, in_x, out_r, in_r, sib_out, sib_in,
    rel_out, rel_in, dir_out, dir_in, fin_out, fin_in, score_buf, gain_col,
    w_sem, x_send, x_recv, g_send, g_recv, s_send, s_recv, c_send, c_recv, r_send, r_recv,
    q_send, q_recv,
):
    seq = lax.axis_index("seq")
    ex = lax.axis_index("exp")
    zz, yy = seq // 4, lax.rem(seq, 4)
    x, c = ex // 2, lax.rem(ex, 2)
    right, left, opp = lax.rem(x + 1, 4), lax.rem(x + 3, 4), lax.rem(x + 2, 4)
    oc = 1 - c

    def seq_peer(k):
        dz, dy = k // 4, lax.rem(k, 4)
        return lax.rem(zz + dz, 4) * 4 + lax.rem(yy + dy, 4)

    def each_peer(step):
        def body(k, carry):
            step(seq_peer(k))
            return carry

        lax.fori_loop(1, OWNERS, body, 0)

    def each_part(step):
        def body(k, carry):
            step(lax.rem(ex + k, 8))
            return carry

        lax.fori_loop(1, 8, body, 0)

    weight_copies = [
        pltpu.make_async_copy(gate_hbm, gate_v, w_sem.at[0]),
        pltpu.make_async_copy(up_hbm, up_v, w_sem.at[1]),
    ] + [
        pltpu.make_async_copy(down_hbm.at[0, :, pl.ds(i * WIDE, WIDE)], down_v.at[i], w_sem.at[2 + i])
        for i in range(CHIPS)
    ]

    barrier = pltpu.get_barrier_semaphore()

    def greet(s, e):
        pl.semaphore_signal(barrier, inc=1, device_id=(s, e), device_id_type=MESH)

    each_peer(lambda peer: greet(peer, ex))
    each_part(lambda peer: greet(seq, peer))
    for copy in weight_copies:
        copy.start()

    lower = seq * CAP
    table = chosen[...]
    begins = jnp.sum((table < lower).astype(jnp.int32), axis=1, keepdims=True)
    mine = jnp.logical_and(table >= lower, table < lower + CAP)
    slots = jnp.where(mine, iota((OWNERS, CAP), 1) - begins, -1)
    local = table - lower
    sub = iota((MOST, CAP), 0)
    lanes = iota((MOST, CAP), 1)
    for e in range(OWNERS):
        hit = slots[e : e + 1, :] == sub
        token = jnp.sum(jnp.where(hit, local[e : e + 1, :] + 1, 0), axis=1, keepdims=True) - 1
        send_m[e * MOST : (e + 1) * MOST, :] = jnp.where(token == lanes, 1.0, 0.0).astype(BF16)

    def slot(owner):
        return pl.ds(pl.multiple_of(owner * MOST, MOST), MOST)

    def x_copy(ch, peer, place):
        return pltpu.make_async_remote_copy(
            src_ref=out_x.at[ch, slot(peer), :],
            dst_ref=in_x.at[ch, slot(place), :],
            send_sem=x_send.at[ch, peer],
            recv_sem=x_recv.at[ch, place],
            device_id=(peer, ex),
            device_id_type=MESH,
        )

    def pack(a, source):
        block = dot(send_m[...], source[...]).astype(BF16)
        out_x[2 * a] = block[:, 0:LANES]
        out_x[2 * a + 1] = block[:, LANES:PART]

    def x_start(ch):
        each_peer(lambda peer: x_copy(ch, peer, seq).start())
        in_x[ch, slot(seq), :] = out_x[ch, slot(seq), :]

    pack(0, tokens)
    pl.semaphore_wait(barrier, OWNERS - 1 + 7)
    x_start(0)
    x_start(1)
    pack(1, grads_in)
    x_start(2)
    x_start(3)

    picked = chosen[pl.ds(seq, 1), :]
    owner_low = iota((OWNERS, CAP), 0) * CAP
    wide = jnp.broadcast_to(picked, (OWNERS, CAP))
    firsts = jnp.sum((wide < owner_low).astype(jnp.int32), axis=1, keepdims=True)
    inside = jnp.logical_and(wide >= owner_low, wide < owner_low + CAP)
    places = jnp.where(inside, iota((OWNERS, CAP), 1) - firsts, -1)
    for g in range(OWNERS // 2):
        block = jnp.concatenate(
            [jnp.where(places[o : o + 1, :] == sub, 1.0, 0.0) for o in (2 * g, 2 * g + 1)], axis=0
        )
        here = slice(g * 2 * MOST, (g + 1) * 2 * MOST)
        pick_t[here, :] = block.astype(BF16)
        pick_m[:, here] = block.T.astype(BF16)
        send_t[:, here] = send_m[here, :].astype(F32).T.astype(BF16)
    gain_col[...] = jnp.broadcast_to(scores[...], (128, CAP)).T

    def region(ch, xx, cc):
        a, f = ch // 2, ch % 2
        return full.at[a, xx, :, pl.ds(pl.multiple_of(cc * PART + f * LANES, LANES), LANES)]

    def g_copy(ch, k):
        f = ch % 2
        view, target = {
            0: (region(ch, x, c), (x, oc)),
            1: (region(ch, x, c), (right, c)),
            2: (region(ch, x, c), (left, c)),
            3: (region(ch, left, c), (x, oc)),
            4: (region(ch, right, c), (x, oc)),
            5: (region(ch, left, c), (right, c)) if f == 0 else (region(ch, right, c), (left, c)),
            6: (region(ch, opp, c), (x, oc)),
        }[k]
        return pltpu.make_async_remote_copy(
            src_ref=view, dst_ref=view, send_sem=g_send.at[ch, k], recv_sem=g_recv.at[ch, k],
            device_id=(seq, target[0] * 2 + target[1]), device_id_type=MESH,
        )

    def g_wait(ch, k):
        g_copy(ch, k).wait_recv()

    def g_start(ch, k):
        g_copy(ch, k).start()

    def compact(ch):
        each_peer(lambda peer: x_copy(ch, peer, peer).wait_recv())
        a, f = ch // 2, ch % 2
        cols = pl.ds(pl.multiple_of(c * PART + f * LANES, LANES), LANES)
        full[a, x, :, cols] = dot(pick_m[...], in_x[ch]).astype(BF16)
        for k in (1, 2, 0) if f == 0 else (2, 1, 0):
            g_start(ch, k)

    def relay(ch):
        for k in (1, 2) if ch % 2 == 0 else (2, 1):
            g_wait(ch, k)
            if k == 1 + ch % 2:
                g_start(ch, 5)
            g_start(ch, 2 + k)

    def relay_opp(ch):
        g_wait(ch, 5)
        g_start(ch, 6)

    def gate_up(xx, first):
        def body(n, carry):
            cols = pl.ds(pl.multiple_of(n * WIDE, WIDE), WIDE)
            for acc, w in ((gate_acc, gate_v), (up_acc, up_v)):
                term = dot(full[0, xx], w[xx, :, cols])
                acc[:, cols] = term if first else acc[:, cols] + term
            return carry

        lax.fori_loop(0, HID // WIDE, body, 0)

    def flip_rows(xx):
        rows_t[xx] = full[0, xx].T

    def scale(xx):
        scaled[xx] = (gain_col[:, 0:1] * full[1, xx].astype(F32)).astype(BF16)

    def back(xx, first):
        def body(n, carry):
            cols = pl.ds(pl.multiple_of(n * WIDE, WIDE), WIDE)
            term = dot_t(full[1, xx], down_v[xx, cols, :])
            back_acc[:, cols] = term if first else back_acc[:, cols] + term
            return carry

        lax.fori_loop(0, HID // WIDE, body, 0)

    def g_wait_both(a, k):
        g_wait(2 * a, k)
        g_wait(2 * a + 1, k)

    compact(0)
    compact(1)
    relay(0)
    for copy in weight_copies:
        copy.wait()
    g_wait_both(0, 0)
    gate_up(x, True)
    compact(2)
    relay(1)
    compact(3)
    g_wait_both(0, 3)
    gate_up(left, False)
    g_wait_both(0, 4)
    gate_up(right, False)
    relay_opp(0)
    relay_opp(1)
    relay(2)
    flip_rows(x)
    g_wait_both(0, 6)
    gate_up(opp, False)
    relay(3)

    def activate(i, carry):
        rows = pl.ds(pl.multiple_of(i * 16, 16), 16)
        pre, up = gate_acc[rows, :], up_acc[rows, :]
        gain = gain_col[rows, 0:1]
        sigma = jax.nn.sigmoid(pre)
        silu = pre * sigma
        hidden[rows, :] = (silu * up).astype(BF16)
        gate_acc[rows, :] = gain * up * sigma * (1.0 + pre * (1.0 - sigma))
        up_acc[rows, :] = gain * silu
        return carry

    lax.fori_loop(0, CAP // 16, activate, 0)
    g_wait_both(1, 0)
    back(x, True)
    g_wait_both(1, 3)
    back(left, False)
    relay_opp(2)
    g_wait_both(1, 4)
    back(right, False)
    flip_rows(left)
    flip_rows(right)
    relay_opp(3)
    flip_rows(opp)
    hidden_t[...] = hidden[...].T
    g_wait_both(1, 6)
    back(opp, False)

    def finish(i, carry):
        rows = pl.ds(pl.multiple_of(i * 16, 16), 16)
        bh = back_acc[rows, :]
        ggp[rows, :] = (bh * gate_acc[rows, :]).astype(BF16)
        gup[rows, :] = (bh * up_acc[rows, :]).astype(BF16)
        return carry

    lax.fori_loop(0, CAP // 16, finish, 0)

    def contrib(xx, cc):
        feats = part_of(cc)
        return dot_t(ggp[...], gate_v[xx, feats, :]) + dot_t(gup[...], up_v[xx, feats, :])

    order = (opp, left, right, x)

    def s_copy(k):
        return pltpu.make_async_remote_copy(
            src_ref=sib_out.at[k], dst_ref=sib_in.at[k], send_sem=s_send.at[k], recv_sem=s_recv.at[k],
            device_id=(seq, x * 2 + oc), device_id_type=MESH,
        )

    def r_copy(f, k):
        src, dst, target = (
            (rel_out.at[f, 0], rel_in.at[f, 0], right),
            (rel_out.at[f, 1], rel_in.at[f, 1], left),
            (dir_out.at[f, 0], dir_in.at[f, 0], left),
            (dir_out.at[f, 1], dir_in.at[f, 1], right),
            (fin_out.at[f, 0], fin_in.at[f, 0], right),
            (fin_out.at[f, 1], fin_in.at[f, 1], left),
        )[k]
        return pltpu.make_async_remote_copy(
            src_ref=src, dst_ref=dst, send_sem=r_send.at[f, k], recv_sem=r_recv.at[f, k],
            device_id=(seq, target * 2 + c), device_id_type=MESH,
        )

    def for_sibling(k):
        sib_out[k] = contrib(order[k], oc).astype(BF16)
        s_copy(k).start()

    def sums(k, f, h):
        cols = k * PART + f * LANES
        return gate_acc[h * HALF : (h + 1) * HALF, cols : cols + LANES]

    def for_chip(k):
        gate_acc[:, k * PART : (k + 1) * PART] = contrib(order[k], c)

    def add_sibling(k):
        s_copy(k).wait_recv()
        here = slice(k * PART, (k + 1) * PART)
        gate_acc[:, here] = gate_acc[:, here] + sib_in[k].astype(F32)

    def send_direct(f, h):
        dir_out[f, h] = sums(1 + h, f, h).astype(BF16)
        r_copy(f, 2 + h).start()

    def send_final(f):
        for h in range(2):
            r_copy(f, h).wait_recv()
            fin_out[f, h] = (sums(2 - h, f, h) + rel_in[f, h].astype(F32)).astype(BF16)
            r_copy(f, 4 + h).start()

    for_sibling(0)
    for_sibling(1)
    for_chip(0)
    add_sibling(0)
    for f in range(2):
        for h in range(2):
            rel_out[f, h] = sums(0, f, h).astype(BF16)
            r_copy(f, h).start()
    for_sibling(2)
    for_chip(1)
    add_sibling(1)
    send_direct(0, 0)
    for_chip(2)
    add_sibling(2)
    send_direct(0, 1)
    for_sibling(3)

    def score_rows(i, carry):
        rows = pl.ds(pl.multiple_of(i * 16, 16), 16)
        prod = hidden[rows, :].astype(F32) * back_acc[rows, :]
        part = prod[:, 0:128]
        for j in range(1, HID // 128):
            part = part + prod[:, j * 128 : (j + 1) * 128]
        back_acc[rows, 0:128] = part
        return carry

    def q_copy(peer, place):
        return pltpu.make_async_remote_copy(
            src_ref=score_buf.at[ex], dst_ref=score_buf.at[place], send_sem=q_send.at[peer], recv_sem=q_recv.at[place],
            device_id=(seq, peer), device_id_type=MESH,
        )

    send_final(0)
    send_direct(1, 0)
    send_direct(1, 1)
    for_chip(3)
    lax.fori_loop(0, CAP // 16, score_rows, 0)
    send_final(1)
    score_part = jnp.sum(back_acc[:, 0:128].T, axis=0, keepdims=True)
    score_buf[ex] = score_part
    each_part(lambda peer: q_copy(peer, ex).start())

    def weight_rows(xx):
        def body(n, carry):
            cols = pl.ds(pl.multiple_of(n * WIDE, WIDE), WIDE)
            here = pl.ds(pl.multiple_of(xx * WIDE, WIDE), WIDE)
            grad_gate[here, cols] = dot(rows_t[xx], ggp[:, cols]).astype(BF16)
            grad_up[here, cols] = dot(rows_t[xx], gup[:, cols]).astype(BF16)
            return carry

        lax.fori_loop(0, HID // WIDE, body, 0)

    def c_copy(f, peer, place):
        return pltpu.make_async_remote_copy(
            src_ref=out_r.at[f, slot(peer), :],
            dst_ref=in_r.at[f, slot(place), :],
            send_sem=c_send.at[f, peer],
            recv_sem=c_recv.at[f, place],
            device_id=(peer, ex),
            device_id_type=MESH,
        )

    def give_back(f):
        for k in (2, 3, 4, 5):
            r_copy(f, k).wait_recv()
        halves = [
            (sums(3, f, h) + fin_in[f, h].astype(F32) + dir_in[f, h].astype(F32)).astype(BF16) for h in range(2)
        ]
        out_r[f] = dot(pick_t[...], jnp.concatenate(halves, axis=0)).astype(BF16)
        each_peer(lambda peer: c_copy(f, peer, seq).start())
        in_r[f, slot(seq), :] = out_r[f, slot(seq), :]

    add_sibling(3)
    weight_rows(x)
    give_back(0)
    weight_rows(left)
    give_back(1)
    weight_rows(right)
    weight_rows(opp)
    for xx in range(CHIPS):
        scale(xx)

    each_part(lambda peer: q_copy(peer, peer).wait_recv())
    total = score_buf[0]
    for i in range(1, 8):
        total = total + score_buf[i]
    score_out[...] = total

    for f in range(2):
        each_peer(lambda peer: c_copy(f, peer, peer).wait_recv())
        tok_out[:, f * LANES : (f + 1) * LANES] = dot(send_t[...], in_r[f]).astype(BF16)

    def sent(peer):
        for ch in range(4):
            x_copy(ch, peer, seq).wait_send()
        for f in range(2):
            c_copy(f, peer, seq).wait_send()

    each_peer(sent)
    each_part(lambda peer: q_copy(peer, ex).wait_send())
    for ch in range(4):
        for k in range(7):
            g_copy(ch, k).wait_send()
    for k in range(4):
        s_copy(k).wait_send()
    for f in range(2):
        for k in range(6):
            r_copy(f, k).wait_send()


def store_kernel(
    tok, score, grad_gate, grad_up, hidden_t, scaled, tok_hbm, score_hbm, gate_hbm, up_hbm, down_hbm, stage, sems
):
    copies = [
        pltpu.make_async_copy(tok, tok_hbm, sems.at[0]),
        pltpu.make_async_copy(score, score_hbm, sems.at[1]),
    ]
    for src, dst in ((grad_gate, gate_hbm), (grad_up, up_hbm)):
        for i in range(CHIPS):
            here = pl.ds(i * WIDE, WIDE)
            copies.append(pltpu.make_async_copy(src.at[here, :], dst.at[here, :], sems.at[len(copies)]))
    for copy in copies:
        copy.start()
    for i in range(CHIPS):

        def body(n, carry):
            here = pl.ds(pl.multiple_of(n * WIDE, WIDE), WIDE)
            stage[i, here, :] = dot(hidden_t[here, :], scaled[i]).astype(BF16)
            return carry

        lax.fori_loop(0, HID // WIDE, body, 0)
        last = pltpu.make_async_copy(stage.at[i], down_hbm.at[:, pl.ds(i * WIDE, WIDE)], sems.at[len(copies)])
        last.start()
        copies.append(last)
    for copy in copies:
        copy.wait()


def shards(tokens, grad_out, chosen, scores, gate_weight, up_weight, down_weight):
    vmem = pl.BlockSpec(memory_space=pltpu.VMEM)
    anyw = pl.BlockSpec(memory_space=pl.ANY)
    shape = jax.ShapeDtypeStruct
    dma = pltpu.SemaphoreType.DMA
    first = (((CAP, PART), BF16), ((1, CAP), F32), ((CHIPS * WIDE, HID), BF16), ((CHIPS * WIDE, HID), BF16))
    left_over = (((HID, CAP), BF16), ((CHIPS, CAP, WIDE), BF16))
    results = first + (((HID, CHIPS * WIDE), BF16),)
    kept = pl.pallas_call(
        layer_kernel,
        out_shape=tuple(pltpu.VMEM(*r) for r in first + left_over),
        in_specs=[vmem] * 4 + [anyw] * 3,
        out_specs=(vmem,) * 6,
        scratch_shapes=[
            pltpu.VMEM((CHIPS, WIDE, HID), BF16),
            pltpu.VMEM((CHIPS, WIDE, HID), BF16),
            pltpu.VMEM((CHIPS, HID, WIDE), BF16),
            pltpu.VMEM((2, CHIPS, CAP, WIDE), BF16),
            pltpu.VMEM((CAP, HID), F32),
            pltpu.VMEM((CAP, HID), F32),
            pltpu.VMEM((CAP, HID), F32),
            pltpu.VMEM((CAP, HID), BF16),
            pltpu.VMEM((CAP, HID), BF16),
            pltpu.VMEM((CAP, HID), BF16),
            pltpu.VMEM((CHIPS, WIDE, CAP), BF16),
            pltpu.VMEM((OWNERS * MOST, CAP), BF16),
            pltpu.VMEM((CAP, OWNERS * MOST), BF16),
            pltpu.VMEM((CAP, OWNERS * MOST), BF16),
            pltpu.VMEM((OWNERS * MOST, CAP), BF16),
            pltpu.VMEM((4, OWNERS * MOST, LANES), BF16),
            pltpu.VMEM((4, OWNERS * MOST, LANES), BF16),
            pltpu.VMEM((2, OWNERS * MOST, LANES), BF16),
            pltpu.VMEM((2, OWNERS * MOST, LANES), BF16),
            pltpu.VMEM((CHIPS, CAP, PART), BF16),
            pltpu.VMEM((CHIPS, CAP, PART), BF16),
        ]
        + [pltpu.VMEM((2, 2, HALF, LANES), BF16)] * 6
        + [
            pltpu.VMEM((8, 1, CAP), F32),
            pltpu.VMEM((CAP, 128), F32),
            dma((2 + CHIPS,)),
            dma((4, OWNERS)),
            dma((4, OWNERS)),
            dma((4, 7)),
            dma((4, 7)),
            dma((4,)),
            dma((4,)),
            dma((2, OWNERS)),
            dma((2, OWNERS)),
            dma((2, 6)),
            dma((2, 6)),
            dma((8,)),
            dma((8,)),
        ],
        compiler_params=pltpu.CompilerParams(
            collective_id=0, has_side_effects=True, vmem_limit_bytes=VMEM_BYTES
        ),
        name="layer",
    )(
        tokens,
        grad_out,
        chosen,
        scores,
        gate_weight.reshape(CHIPS, WIDE, HID),
        up_weight.reshape(CHIPS, WIDE, HID),
        down_weight,
    )
    tok, score, grad_gate, grad_up, grad_down = pl.pallas_call(
        store_kernel,
        out_shape=tuple(shape(*r) for r in results),
        in_specs=[vmem] * 6,
        out_specs=(anyw,) * 5,
        scratch_shapes=[pltpu.VMEM((CHIPS, HID, WIDE), BF16), dma((16,))],
        compiler_params=pltpu.CompilerParams(vmem_limit_bytes=8 * 1024 * 1024),
        name="store",
    )(*[pltpu.with_memory_space_constraint(k, pltpu.VMEM) for k in kept])
    return tok, score, grad_gate[None], grad_up[None], grad_down[None]


def solution(mesh):
    in_specs = (
        P("seq", "exp"),
        P("seq", "exp"),
        P(),
        P("seq", None),
        P("seq", None, "exp"),
        P("seq", None, "exp"),
        P("seq", "exp", None),
    )
    out_specs = (
        P("seq", "exp"),
        P("seq", None),
        P("seq", None, "exp"),
        P("seq", None, "exp"),
        P("seq", "exp", None),
    )
    return jax.shard_map(shards, mesh=mesh, in_specs=in_specs, out_specs=out_specs, check_vma=False)
```

```python
import functools

import jax
import jax.numpy as jnp
from jax import lax
from jax.experimental import pallas as pl
from jax.experimental.pallas import tpu as pltpu
from jax.sharding import PartitionSpec as P

MESH = pl.DeviceIdType.MESH
BF16 = jnp.bfloat16
F32 = jnp.float32

OWNERS = 16
MOST = 64
CAP = 512
PART = 256
CHIPS = 4
WIDE = 512
HID = 1024
LANES = 128
HALF = CAP // 2
VMEM_BYTES = 50 * 1024 * 1024


def dot(a, b):
    return jnp.dot(a, b, preferred_element_type=F32)


def dot_t(a, b):
    return lax.dot_general(a, b, (((1,), (1,)), ((), ())), preferred_element_type=F32)


def iota(shape, axis):
    return lax.broadcasted_iota(jnp.int32, shape, axis)


def part_of(c):
    return pl.ds(pl.multiple_of(c * PART, PART), PART)


def layer_kernel(
    tokens, grads_in, chosen, scores, gate_hbm, up_hbm, down_hbm,
    tok_out, score_out, grad_gate, grad_up, hidden_t, scaled,
    gate_v, up_v, down_v, full, gate_acc, up_acc, back_acc, hidden, ggp, gup,
    rows_t, send_m, send_t, pick_m, pick_t, out_x, in_x, out_r, in_r, sib_out, sib_in,
    rel_out, rel_in, dir_out, dir_in, fin_out, fin_in, score_buf, gain_col,
    w_sem, x_send, x_recv, g_send, g_recv, s_send, s_recv, c_send, c_recv, r_send, r_recv,
    q_send, q_recv,
):
    seq = lax.axis_index("seq")
    ex = lax.axis_index("exp")
    zz, yy = seq // 4, lax.rem(seq, 4)
    x, c = ex // 2, lax.rem(ex, 2)
    right, left, opp = lax.rem(x + 1, 4), lax.rem(x + 3, 4), lax.rem(x + 2, 4)
    oc = 1 - c

    def seq_peer(k):
        dz, dy = k // 4, lax.rem(k, 4)
        return lax.rem(zz + dz, 4) * 4 + lax.rem(yy + dy, 4)

    def each_peer(step):
        def body(k, carry):
            step(seq_peer(k))
            return carry

        lax.fori_loop(1, OWNERS, body, 0)

    def each_part(step):
        def body(k, carry):
            step(lax.rem(ex + k, 8))
            return carry

        lax.fori_loop(1, 8, body, 0)

    weight_copies = [
        pltpu.make_async_copy(gate_hbm, gate_v, w_sem.at[0]),
        pltpu.make_async_copy(up_hbm, up_v, w_sem.at[1]),
    ] + [
        pltpu.make_async_copy(down_hbm.at[0, :, pl.ds(i * WIDE, WIDE)], down_v.at[i], w_sem.at[2 + i])
        for i in range(CHIPS)
    ]

    barrier = pltpu.get_barrier_semaphore()

    def greet(s, e):
        pl.semaphore_signal(barrier, inc=1, device_id=(s, e), device_id_type=MESH)

    each_peer(lambda peer: greet(peer, ex))
    each_part(lambda peer: greet(seq, peer))
    for copy in weight_copies:
        copy.start()

    lower = seq * CAP
    table = chosen[...]
    begins = jnp.sum((table < lower).astype(jnp.int32), axis=1, keepdims=True)
    mine = jnp.logical_and(table >= lower, table < lower + CAP)
    slots = jnp.where(mine, iota((OWNERS, CAP), 1) - begins, -1)
    local = table - lower
    sub = iota((MOST, CAP), 0)
    lanes = iota((MOST, CAP), 1)
    for e in range(OWNERS):
        hit = slots[e : e + 1, :] == sub
        token = jnp.sum(jnp.where(hit, local[e : e + 1, :] + 1, 0), axis=1, keepdims=True) - 1
        send_m[e * MOST : (e + 1) * MOST, :] = jnp.where(token == lanes, 1.0, 0.0).astype(BF16)

    def slot(owner):
        return pl.ds(pl.multiple_of(owner * MOST, MOST), MOST)

    def x_copy(ch, peer, place):
        return pltpu.make_async_remote_copy(
            src_ref=out_x.at[ch, slot(peer), :],
            dst_ref=in_x.at[ch, slot(place), :],
            send_sem=x_send.at[ch, peer],
            recv_sem=x_recv.at[ch, place],
            device_id=(peer, ex),
            device_id_type=MESH,
        )

    def pack(a, source):
        block = dot(send_m[...], source[...]).astype(BF16)
        out_x[2 * a] = block[:, 0:LANES]
        out_x[2 * a + 1] = block[:, LANES:PART]

    def x_start(ch):
        each_peer(lambda peer: x_copy(ch, peer, seq).start())
        in_x[ch, slot(seq), :] = out_x[ch, slot(seq), :]

    pack(0, tokens)
    pl.semaphore_wait(barrier, OWNERS - 1 + 7)
    x_start(0)
    x_start(1)
    picked = chosen[pl.ds(seq, 1), :]
    owner_low = iota((OWNERS, CAP), 0) * CAP
    wide = jnp.broadcast_to(picked, (OWNERS, CAP))
    firsts = jnp.sum((wide < owner_low).astype(jnp.int32), axis=1, keepdims=True)
    inside = jnp.logical_and(wide >= owner_low, wide < owner_low + CAP)
    places = jnp.where(inside, iota((OWNERS, CAP), 1) - firsts, -1)
    for g in range(OWNERS // 2):
        block = jnp.concatenate(
            [jnp.where(places[o : o + 1, :] == sub, 1.0, 0.0) for o in (2 * g, 2 * g + 1)], axis=0
        )
        here = slice(g * 2 * MOST, (g + 1) * 2 * MOST)
        pick_t[here, :] = block.astype(BF16)
        pick_m[:, here] = block.T.astype(BF16)
    pack(1, grads_in)
    x_start(2)
    x_start(3)
    gain_col[...] = jnp.broadcast_to(scores[...], (128, CAP)).T
    for g in range(OWNERS // 2):
        here = slice(g * 2 * MOST, (g + 1) * 2 * MOST)
        send_t[:, here] = send_m[here, :].astype(F32).T.astype(BF16)

    def region(ch, xx, cc):
        a, f = ch // 2, ch % 2
        return full.at[a, xx, :, pl.ds(pl.multiple_of(cc * PART + f * LANES, LANES), LANES)]

    def g_copy(ch, k):
        f = ch % 2
        view, target = {
            0: (region(ch, x, c), (x, oc)),
            1: (region(ch, x, c), (right, c)),
            2: (region(ch, x, c), (left, c)),
            3: (region(ch, left, c), (x, oc)),
            4: (region(ch, right, c), (x, oc)),
            5: (region(ch, left, c), (right, c)) if f == 0 else (region(ch, right, c), (left, c)),
            6: (region(ch, opp, c), (x, oc)),
        }[k]
        return pltpu.make_async_remote_copy(
            src_ref=view, dst_ref=view, send_sem=g_send.at[ch, k], recv_sem=g_recv.at[ch, k],
            device_id=(seq, target[0] * 2 + target[1]), device_id_type=MESH,
        )

    def g_wait(ch, k):
        g_copy(ch, k).wait_recv()

    def g_start(ch, k):
        g_copy(ch, k).start()

    def compact(ch):
        each_peer(lambda peer: x_copy(ch, peer, peer).wait_recv())
        a, f = ch // 2, ch % 2
        cols = pl.ds(pl.multiple_of(c * PART + f * LANES, LANES), LANES)
        full[a, x, :, cols] = dot(pick_m[...], in_x[ch]).astype(BF16)
        for k in (1, 2, 0) if f == 0 else (2, 1, 0):
            g_start(ch, k)

    def relay(ch):
        for k in (1, 2) if ch % 2 == 0 else (2, 1):
            g_wait(ch, k)
            if k == 1 + ch % 2:
                g_start(ch, 5)
            g_start(ch, 2 + k)

    def relay_opp(ch):
        g_wait(ch, 5)
        g_start(ch, 6)

    def gate_up(xx, first):
        def body(n):
            cols = slice(n * WIDE, (n + 1) * WIDE)
            for acc, w in ((gate_acc, gate_v), (up_acc, up_v)):
                term = dot(full[0, xx], w[xx, :, cols])
                acc[:, cols] = term if first else acc[:, cols] + term

        for n in range(HID // WIDE):
            body(n)

    def flip_rows(xx):
        rows_t[xx] = full[0, xx].T

    def scale(xx):
        scaled[xx] = (gain_col[:, 0:1] * full[1, xx].astype(F32)).astype(BF16)

    def back(xx, first):
        def body(n):
            cols = slice(n * WIDE, (n + 1) * WIDE)
            term = dot_t(full[1, xx], down_v[xx, cols, :])
            back_acc[:, cols] = term if first else back_acc[:, cols] + term

        for n in range(HID // WIDE):
            body(n)

    def g_wait_both(a, k):
        g_wait(2 * a, k)
        g_wait(2 * a + 1, k)

    compact(0)
    compact(1)
    for copy in weight_copies:
        copy.wait()
    g_wait_both(0, 0)
    gate_up(x, True)
    relay(0)
    compact(2)
    relay(1)
    compact(3)
    g_wait_both(0, 3)
    gate_up(left, False)
    g_wait_both(0, 4)
    gate_up(right, False)
    relay_opp(0)
    relay_opp(1)
    relay(2)
    flip_rows(x)
    g_wait_both(0, 6)
    gate_up(opp, False)
    relay(3)

    def activate(i, carry):
        rows = pl.ds(pl.multiple_of(i * 16, 16), 16)
        pre, up = gate_acc[rows, :], up_acc[rows, :]
        gain = gain_col[rows, 0:1]
        sigma = jax.nn.sigmoid(pre)
        silu = pre * sigma
        hidden[rows, :] = (silu * up).astype(BF16)
        gate_acc[rows, :] = gain * up * sigma * (1.0 + pre * (1.0 - sigma))
        up_acc[rows, :] = gain * silu
        return carry

    lax.fori_loop(0, CAP // 16, activate, 0, unroll=2)
    g_wait_both(1, 0)
    back(x, True)
    g_wait_both(1, 3)
    back(left, False)
    relay_opp(2)
    g_wait_both(1, 4)
    back(right, False)
    flip_rows(left)
    flip_rows(right)
    relay_opp(3)
    flip_rows(opp)
    hidden_t[...] = hidden[...].T
    g_wait_both(1, 6)
    back(opp, False)

    def finish(i, carry):
        rows = pl.ds(pl.multiple_of(i * 16, 16), 16)
        bh = back_acc[rows, :]
        ggp[rows, :] = (bh * gate_acc[rows, :]).astype(BF16)
        gup[rows, :] = (bh * up_acc[rows, :]).astype(BF16)
        return carry

    lax.fori_loop(0, CAP // 16, finish, 0, unroll=4)

    def contrib(xx, cc):
        feats = part_of(cc)
        return dot_t(ggp[...], gate_v[xx, feats, :]) + dot_t(gup[...], up_v[xx, feats, :])

    order = (opp, left, right, x)

    def s_copy(k):
        return pltpu.make_async_remote_copy(
            src_ref=sib_out.at[k], dst_ref=sib_in.at[k], send_sem=s_send.at[k], recv_sem=s_recv.at[k],
            device_id=(seq, x * 2 + oc), device_id_type=MESH,
        )

    def r_copy(f, k):
        src, dst, target = (
            (rel_out.at[f, 0], rel_in.at[f, 0], right),
            (rel_out.at[f, 1], rel_in.at[f, 1], left),
            (dir_out.at[f, 0], dir_in.at[f, 0], left),
            (dir_out.at[f, 1], dir_in.at[f, 1], right),
            (fin_out.at[f, 0], fin_in.at[f, 0], right),
            (fin_out.at[f, 1], fin_in.at[f, 1], left),
        )[k]
        return pltpu.make_async_remote_copy(
            src_ref=src, dst_ref=dst, send_sem=r_send.at[f, k], recv_sem=r_recv.at[f, k],
            device_id=(seq, target * 2 + c), device_id_type=MESH,
        )

    def for_sibling(k):
        sib_out[k] = contrib(order[k], oc).astype(BF16)
        s_copy(k).start()

    def sums(k, f, h):
        cols = k * PART + f * LANES
        return gate_acc[h * HALF : (h + 1) * HALF, cols : cols + LANES]

    def for_chip(k):
        gate_acc[:, k * PART : (k + 1) * PART] = contrib(order[k], c)

    def add_sibling(k):
        s_copy(k).wait_recv()
        here = slice(k * PART, (k + 1) * PART)
        gate_acc[:, here] = gate_acc[:, here] + sib_in[k].astype(F32)

    def send_direct(f, h):
        dir_out[f, h] = sums(1 + h, f, h).astype(BF16)
        r_copy(f, 2 + h).start()

    def send_final(f):
        for h in range(2):
            r_copy(f, h).wait_recv()
            fin_out[f, h] = (sums(2 - h, f, h) + rel_in[f, h].astype(F32)).astype(BF16)
            r_copy(f, 4 + h).start()

    for_sibling(0)
    for_sibling(1)
    for_chip(0)
    add_sibling(0)
    for f in range(2):
        for h in range(2):
            rel_out[f, h] = sums(0, f, h).astype(BF16)
            r_copy(f, h).start()
    for_sibling(2)
    for_chip(1)
    add_sibling(1)
    send_direct(0, 0)
    for_chip(2)
    add_sibling(2)
    send_direct(0, 1)
    for_sibling(3)

    def score_rows(i, carry):
        rows = pl.ds(pl.multiple_of(i * 16, 16), 16)
        prod = hidden[rows, :].astype(F32) * back_acc[rows, :]
        part = prod[:, 0:128]
        for j in range(1, HID // 128):
            part = part + prod[:, j * 128 : (j + 1) * 128]
        back_acc[rows, 0:128] = part
        return carry

    def q_copy(peer, place):
        return pltpu.make_async_remote_copy(
            src_ref=score_buf.at[ex], dst_ref=score_buf.at[place], send_sem=q_send.at[peer], recv_sem=q_recv.at[place],
            device_id=(seq, peer), device_id_type=MESH,
        )

    send_final(0)
    send_direct(1, 0)
    send_direct(1, 1)
    for_chip(3)
    lax.fori_loop(0, CAP // 16, score_rows, 0, unroll=2)
    send_final(1)
    score_part = jnp.sum(back_acc[:, 0:128].T, axis=0, keepdims=True)
    score_buf[ex] = score_part
    each_part(lambda peer: q_copy(peer, ex).start())

    def weight_rows(xx):
        def body(n):
            cols = slice(n * WIDE, (n + 1) * WIDE)
            here = pl.ds(pl.multiple_of(xx * WIDE, WIDE), WIDE)
            grad_gate[here, cols] = dot(rows_t[xx], ggp[:, cols]).astype(BF16)
            grad_up[here, cols] = dot(rows_t[xx], gup[:, cols]).astype(BF16)

        for n in range(HID // WIDE):
            body(n)

    def c_copy(f, peer, place):
        return pltpu.make_async_remote_copy(
            src_ref=out_r.at[f, slot(peer), :],
            dst_ref=in_r.at[f, slot(place), :],
            send_sem=c_send.at[f, peer],
            recv_sem=c_recv.at[f, place],
            device_id=(peer, ex),
            device_id_type=MESH,
        )

    def give_back(f):
        for k in (2, 3, 4, 5):
            r_copy(f, k).wait_recv()
        halves = [
            (sums(3, f, h) + fin_in[f, h].astype(F32) + dir_in[f, h].astype(F32)).astype(BF16) for h in range(2)
        ]
        out_r[f] = dot(pick_t[...], jnp.concatenate(halves, axis=0)).astype(BF16)
        each_peer(lambda peer: c_copy(f, peer, seq).start())
        in_r[f, slot(seq), :] = out_r[f, slot(seq), :]

    add_sibling(3)
    weight_rows(x)
    give_back(0)
    weight_rows(left)
    give_back(1)
    weight_rows(right)
    weight_rows(opp)
    for xx in range(CHIPS):
        scale(xx)

    each_peer(lambda peer: [x_copy(ch, peer, seq).wait_send() for ch in range(4)])
    each_part(lambda peer: q_copy(peer, ex).wait_send())
    for ch in range(4):
        for k in range(7):
            g_copy(ch, k).wait_send()
    for k in range(4):
        s_copy(k).wait_send()
    for f in range(2):
        for k in range(6):
            r_copy(f, k).wait_send()

    each_part(lambda peer: q_copy(peer, peer).wait_recv())
    total = score_buf[0]
    for i in range(1, 8):
        total = total + score_buf[i]
    score_out[...] = total

    for f in range(2):
        each_peer(lambda peer: c_copy(f, peer, peer).wait_recv())
        tok_out[:, f * LANES : (f + 1) * LANES] = dot(send_t[...], in_r[f]).astype(BF16)

    each_peer(lambda peer: [c_copy(f, peer, seq).wait_send() for f in range(2)])


def store_kernel(
    tok, score, grad_gate, grad_up, hidden_t, scaled, tok_hbm, score_hbm, gate_hbm, up_hbm, down_hbm, stage, sems
):
    copies = [
        pltpu.make_async_copy(tok, tok_hbm, sems.at[0]),
        pltpu.make_async_copy(score, score_hbm, sems.at[1]),
    ]
    for src, dst in ((grad_gate, gate_hbm), (grad_up, up_hbm)):
        for i in range(CHIPS):
            here = pl.ds(i * WIDE, WIDE)
            copies.append(pltpu.make_async_copy(src.at[here, :], dst.at[here, :], sems.at[len(copies)]))
    for copy in copies:
        copy.start()
    for i in range(CHIPS):

        def body(n, carry):
            here = pl.ds(pl.multiple_of(n * WIDE, WIDE), WIDE)
            stage[i, here, :] = dot(hidden_t[here, :], scaled[i]).astype(BF16)
            return carry

        lax.fori_loop(0, HID // WIDE, body, 0)
        last = pltpu.make_async_copy(stage.at[i], down_hbm.at[:, pl.ds(i * WIDE, WIDE)], sems.at[len(copies)])
        last.start()
        copies.append(last)
    for copy in copies:
        copy.wait()


def shards(tokens, grad_out, chosen, scores, gate_weight, up_weight, down_weight):
    vmem = pl.BlockSpec(memory_space=pltpu.VMEM)
    anyw = pl.BlockSpec(memory_space=pl.ANY)
    shape = jax.ShapeDtypeStruct
    dma = pltpu.SemaphoreType.DMA
    first = (((CAP, PART), BF16), ((1, CAP), F32), ((CHIPS * WIDE, HID), BF16), ((CHIPS * WIDE, HID), BF16))
    left_over = (((HID, CAP), BF16), ((CHIPS, CAP, WIDE), BF16))
    results = first + (((HID, CHIPS * WIDE), BF16),)
    kept = pl.pallas_call(
        layer_kernel,
        out_shape=tuple(pltpu.VMEM(*r) for r in first + left_over),
        in_specs=[vmem] * 4 + [anyw] * 3,
        out_specs=(vmem,) * 6,
        scratch_shapes=[
            pltpu.VMEM((CHIPS, WIDE, HID), BF16),
            pltpu.VMEM((CHIPS, WIDE, HID), BF16),
            pltpu.VMEM((CHIPS, HID, WIDE), BF16),
            pltpu.VMEM((2, CHIPS, CAP, WIDE), BF16),
            pltpu.VMEM((CAP, HID), F32),
            pltpu.VMEM((CAP, HID), F32),
            pltpu.VMEM((CAP, HID), F32),
            pltpu.VMEM((CAP, HID), BF16),
            pltpu.VMEM((CAP, HID), BF16),
            pltpu.VMEM((CAP, HID), BF16),
            pltpu.VMEM((CHIPS, WIDE, CAP), BF16),
            pltpu.VMEM((OWNERS * MOST, CAP), BF16),
            pltpu.VMEM((CAP, OWNERS * MOST), BF16),
            pltpu.VMEM((CAP, OWNERS * MOST), BF16),
            pltpu.VMEM((OWNERS * MOST, CAP), BF16),
            pltpu.VMEM((4, OWNERS * MOST, LANES), BF16),
            pltpu.VMEM((4, OWNERS * MOST, LANES), BF16),
            pltpu.VMEM((2, OWNERS * MOST, LANES), BF16),
            pltpu.VMEM((2, OWNERS * MOST, LANES), BF16),
            pltpu.VMEM((CHIPS, CAP, PART), BF16),
            pltpu.VMEM((CHIPS, CAP, PART), BF16),
        ]
        + [pltpu.VMEM((2, 2, HALF, LANES), BF16)] * 6
        + [
            pltpu.VMEM((8, 1, CAP), F32),
            pltpu.VMEM((CAP, 128), F32),
            dma((2 + CHIPS,)),
            dma((4, OWNERS)),
            dma((4, OWNERS)),
            dma((4, 7)),
            dma((4, 7)),
            dma((4,)),
            dma((4,)),
            dma((2, OWNERS)),
            dma((2, OWNERS)),
            dma((2, 6)),
            dma((2, 6)),
            dma((8,)),
            dma((8,)),
        ],
        compiler_params=pltpu.CompilerParams(
            collective_id=0, has_side_effects=True, vmem_limit_bytes=VMEM_BYTES
        ),
        name="layer",
    )(
        tokens,
        grad_out,
        chosen,
        scores,
        gate_weight.reshape(CHIPS, WIDE, HID),
        up_weight.reshape(CHIPS, WIDE, HID),
        down_weight,
    )
    tok, score, grad_gate, grad_up, grad_down = pl.pallas_call(
        store_kernel,
        out_shape=tuple(shape(*r) for r in results),
        in_specs=[vmem] * 6,
        out_specs=(anyw,) * 5,
        scratch_shapes=[pltpu.VMEM((CHIPS, HID, WIDE), BF16), dma((16,))],
        compiler_params=pltpu.CompilerParams(vmem_limit_bytes=8 * 1024 * 1024),
        name="store",
    )(*[pltpu.with_memory_space_constraint(k, pltpu.VMEM) for k in kept])
    return tok, score, grad_gate[None], grad_up[None], grad_down[None]


def solution(mesh):
    in_specs = (
        P("seq", "exp"),
        P("seq", "exp"),
        P(),
        P("seq", None),
        P("seq", None, "exp"),
        P("seq", None, "exp"),
        P("seq", "exp", None),
    )
    out_specs = (
        P("seq", "exp"),
        P("seq", None),
        P("seq", None, "exp"),
        P("seq", None, "exp"),
        P("seq", "exp", None),
    )
    return jax.shard_map(shards, mesh=mesh, in_specs=in_specs, out_specs=out_specs, check_vma=False)
```

```python
import functools

import jax
import jax.numpy as jnp
from jax import lax
from jax.experimental import pallas as pl
from jax.experimental.pallas import tpu as pltpu
from jax.sharding import PartitionSpec as P

MESH = pl.DeviceIdType.MESH
BF16 = jnp.bfloat16
F32 = jnp.float32

OWNERS = 16
MOST = 64
CAP = 512
PART = 256
CHIPS = 4
WIDE = 512
HID = 1024
LANES = 128
HALF = CAP // 2
VMEM_BYTES = 50 * 1024 * 1024


def dot(a, b):
    return jnp.dot(a, b, preferred_element_type=F32)


def dot_t(a, b):
    return lax.dot_general(a, b, (((1,), (1,)), ((), ())), preferred_element_type=F32)


def iota(shape, axis):
    return lax.broadcasted_iota(jnp.int32, shape, axis)


def part_of(c):
    return pl.ds(pl.multiple_of(c * PART, PART), PART)


def layer_kernel(
    tokens, grads_in, chosen, scores, gate_hbm, up_hbm, down_hbm,
    tok_out, score_out, grad_gate, grad_up, hidden_t, scaled,
    gate_v, up_v, down_v, full, gate_acc, up_acc, back_acc, hidden, ggp, gup,
    rows_t, send_m, send_t, pick_m, pick_t, out_x, in_x, out_r, in_r, sib_out, sib_in,
    rel_out, rel_in, dir_out, dir_in, fin_out, fin_in, score_buf, gain_col,
    w_sem, x_send, x_recv, g_send, g_recv, s_send, s_recv, c_send, c_recv, r_send, r_recv,
    q_send, q_recv,
):
    seq = lax.axis_index("seq")
    ex = lax.axis_index("exp")
    zz, yy = seq // 4, lax.rem(seq, 4)
    x, c = ex // 2, lax.rem(ex, 2)
    right, left, opp = lax.rem(x + 1, 4), lax.rem(x + 3, 4), lax.rem(x + 2, 4)
    oc = 1 - c

    def seq_peer(k):
        dz, dy = k // 4, lax.rem(k, 4)
        return lax.rem(zz + dz, 4) * 4 + lax.rem(yy + dy, 4)

    def each_peer(step):
        def body(k, carry):
            step(seq_peer(k))
            return carry

        lax.fori_loop(1, OWNERS, body, 0)

    def each_part(step):
        def body(k, carry):
            step(lax.rem(ex + k, 8))
            return carry

        lax.fori_loop(1, 8, body, 0)

    weight_copies = [
        pltpu.make_async_copy(gate_hbm, gate_v, w_sem.at[0]),
        pltpu.make_async_copy(up_hbm, up_v, w_sem.at[1]),
    ] + [
        pltpu.make_async_copy(down_hbm.at[0, :, pl.ds(i * WIDE, WIDE)], down_v.at[i], w_sem.at[2 + i])
        for i in range(CHIPS)
    ]

    barrier = pltpu.get_barrier_semaphore()

    def greet(s, e):
        pl.semaphore_signal(barrier, inc=1, device_id=(s, e), device_id_type=MESH)

    each_peer(lambda peer: greet(peer, ex))
    each_part(lambda peer: greet(seq, peer))
    for copy in weight_copies:
        copy.start()

    lower = seq * CAP
    table = chosen[...]
    begins = jnp.sum((table < lower).astype(jnp.int32), axis=1, keepdims=True)
    mine = jnp.logical_and(table >= lower, table < lower + CAP)
    slots = jnp.where(mine, iota((OWNERS, CAP), 1) - begins, -1)
    local = table - lower
    sub = iota((MOST, CAP), 0)
    lanes = iota((MOST, CAP), 1)
    for e in range(OWNERS):
        hit = slots[e : e + 1, :] == sub
        token = jnp.sum(jnp.where(hit, local[e : e + 1, :] + 1, 0), axis=1, keepdims=True) - 1
        send_m[e * MOST : (e + 1) * MOST, :] = jnp.where(token == lanes, 1.0, 0.0).astype(BF16)

    def slot(owner):
        return pl.ds(pl.multiple_of(owner * MOST, MOST), MOST)

    def x_copy(ch, peer, place):
        return pltpu.make_async_remote_copy(
            src_ref=out_x.at[ch, slot(peer), :],
            dst_ref=in_x.at[ch, slot(place), :],
            send_sem=x_send.at[ch, peer],
            recv_sem=x_recv.at[ch, place],
            device_id=(peer, ex),
            device_id_type=MESH,
        )

    def pack(a, source):
        block = dot(send_m[...], source[...]).astype(BF16)
        out_x[2 * a] = block[:, 0:LANES]
        out_x[2 * a + 1] = block[:, LANES:PART]

    def x_start(ch):
        each_peer(lambda peer: x_copy(ch, peer, seq).start())
        in_x[ch, slot(seq), :] = out_x[ch, slot(seq), :]

    pack(0, tokens)
    pl.semaphore_wait(barrier, OWNERS - 1 + 7)
    x_start(0)
    x_start(1)
    picked = chosen[pl.ds(seq, 1), :]
    owner_low = iota((OWNERS, CAP), 0) * CAP
    wide = jnp.broadcast_to(picked, (OWNERS, CAP))
    firsts = jnp.sum((wide < owner_low).astype(jnp.int32), axis=1, keepdims=True)
    inside = jnp.logical_and(wide >= owner_low, wide < owner_low + CAP)
    places = jnp.where(inside, iota((OWNERS, CAP), 1) - firsts, -1)
    for g in range(OWNERS // 2):
        block = jnp.concatenate(
            [jnp.where(places[o : o + 1, :] == sub, 1.0, 0.0) for o in (2 * g, 2 * g + 1)], axis=0
        )
        here = slice(g * 2 * MOST, (g + 1) * 2 * MOST)
        pick_t[here, :] = block.astype(BF16)
        pick_m[:, here] = block.T.astype(BF16)
    pack(1, grads_in)
    x_start(2)
    x_start(3)
    gain_col[...] = jnp.broadcast_to(scores[...], (128, CAP)).T
    for g in range(OWNERS // 2):
        here = slice(g * 2 * MOST, (g + 1) * 2 * MOST)
        send_t[:, here] = send_m[here, :].astype(F32).T.astype(BF16)

    def region(ch, xx, cc):
        a, f = ch // 2, ch % 2
        return full.at[a, xx, :, pl.ds(pl.multiple_of(cc * PART + f * LANES, LANES), LANES)]

    def g_copy(ch, k):
        f = ch % 2
        view, target = {
            0: (region(ch, x, c), (x, oc)),
            1: (region(ch, x, c), (right, c)),
            2: (region(ch, x, c), (left, c)),
            3: (region(ch, left, c), (x, oc)),
            4: (region(ch, right, c), (x, oc)),
            5: (region(ch, left, c), (right, c)) if f == 0 else (region(ch, right, c), (left, c)),
            6: (region(ch, opp, c), (x, oc)),
        }[k]
        return pltpu.make_async_remote_copy(
            src_ref=view, dst_ref=view, send_sem=g_send.at[ch, k], recv_sem=g_recv.at[ch, k],
            device_id=(seq, target[0] * 2 + target[1]), device_id_type=MESH,
        )

    def g_wait(ch, k):
        g_copy(ch, k).wait_recv()

    def g_start(ch, k):
        g_copy(ch, k).start()

    def compact(ch):
        each_peer(lambda peer: x_copy(ch, peer, peer).wait_recv())
        a, f = ch // 2, ch % 2
        cols = pl.ds(pl.multiple_of(c * PART + f * LANES, LANES), LANES)
        full[a, x, :, cols] = dot(pick_m[...], in_x[ch]).astype(BF16)
        for k in (1, 2, 0) if f == 0 else (2, 1, 0):
            g_start(ch, k)

    def relay(ch):
        for k in (1, 2) if ch % 2 == 0 else (2, 1):
            g_wait(ch, k)
            if k == 1 + ch % 2:
                g_start(ch, 5)
            g_start(ch, 2 + k)

    def relay_opp(ch):
        g_wait(ch, 5)
        g_start(ch, 6)

    def gate_up(xx, first):
        def body(n):
            cols = slice(n * WIDE, (n + 1) * WIDE)
            for acc, w in ((gate_acc, gate_v), (up_acc, up_v)):
                term = dot(full[0, xx], w[xx, :, cols])
                acc[:, cols] = term if first else acc[:, cols] + term

        for n in range(HID // WIDE):
            body(n)

    def flip_rows(xx):
        rows_t[xx] = full[0, xx].T

    def scale(xx):
        scaled[xx] = (gain_col[:, 0:1] * full[1, xx].astype(F32)).astype(BF16)

    def back_part(xx, cc):
        for n in range(HID // WIDE):
            cols = slice(n * WIDE, (n + 1) * WIDE)
            feats = part_of(cc)
            back_acc[:, cols] = back_acc[:, cols] + dot_t(full[1, xx, :, feats], down_v[xx, cols, feats])

    def back(xx, first):
        def body(n):
            cols = slice(n * WIDE, (n + 1) * WIDE)
            term = dot_t(full[1, xx], down_v[xx, cols, :])
            back_acc[:, cols] = term if first else back_acc[:, cols] + term

        for n in range(HID // WIDE):
            body(n)

    def g_wait_both(a, k):
        g_wait(2 * a, k)
        g_wait(2 * a + 1, k)

    compact(0)
    compact(1)
    for copy in weight_copies:
        copy.wait()
    g_wait_both(0, 0)
    gate_up(x, True)
    relay(0)
    compact(2)
    relay(1)
    compact(3)
    g_wait_both(0, 3)
    gate_up(left, False)
    g_wait_both(0, 4)
    gate_up(right, False)
    relay_opp(0)
    relay_opp(1)
    relay(2)
    flip_rows(x)
    g_wait_both(0, 6)
    gate_up(opp, False)
    relay(3)

    def activate(i, carry):
        rows = pl.ds(pl.multiple_of(i * 16, 16), 16)
        pre, up = gate_acc[rows, :], up_acc[rows, :]
        gain = gain_col[rows, 0:1]
        sigma = jax.nn.sigmoid(pre)
        silu = pre * sigma
        hidden[rows, :] = (silu * up).astype(BF16)
        gate_acc[rows, :] = gain * up * sigma * (1.0 + pre * (1.0 - sigma))
        up_acc[rows, :] = gain * silu
        return carry

    lax.fori_loop(0, CAP // 16, activate, 0, unroll=2)
    g_wait_both(1, 0)
    back(x, True)
    g_wait_both(1, 3)
    back(left, False)
    relay_opp(2)
    g_wait_both(1, 4)
    back(right, False)
    flip_rows(left)
    flip_rows(right)
    relay_opp(3)
    back_part(opp, c)
    flip_rows(opp)
    g_wait_both(1, 6)
    back_part(opp, oc)

    def finish(i, carry):
        rows = pl.ds(pl.multiple_of(i * 16, 16), 16)
        bh = back_acc[rows, :]
        ggp[rows, :] = (bh * gate_acc[rows, :]).astype(BF16)
        gup[rows, :] = (bh * up_acc[rows, :]).astype(BF16)
        return carry

    lax.fori_loop(0, CAP // 16, finish, 0, unroll=4)

    def contrib(xx, cc):
        feats = part_of(cc)
        return dot_t(ggp[...], gate_v[xx, feats, :]) + dot_t(gup[...], up_v[xx, feats, :])

    order = (opp, left, right, x)

    def s_copy(k):
        return pltpu.make_async_remote_copy(
            src_ref=sib_out.at[k], dst_ref=sib_in.at[k], send_sem=s_send.at[k], recv_sem=s_recv.at[k],
            device_id=(seq, x * 2 + oc), device_id_type=MESH,
        )

    def r_copy(f, k):
        src, dst, target = (
            (rel_out.at[f, 0], rel_in.at[f, 0], right),
            (rel_out.at[f, 1], rel_in.at[f, 1], left),
            (dir_out.at[f, 0], dir_in.at[f, 0], left),
            (dir_out.at[f, 1], dir_in.at[f, 1], right),
            (fin_out.at[f, 0], fin_in.at[f, 0], right),
            (fin_out.at[f, 1], fin_in.at[f, 1], left),
        )[k]
        return pltpu.make_async_remote_copy(
            src_ref=src, dst_ref=dst, send_sem=r_send.at[f, k], recv_sem=r_recv.at[f, k],
            device_id=(seq, target * 2 + c), device_id_type=MESH,
        )

    def for_sibling(k):
        sib_out[k] = contrib(order[k], oc).astype(BF16)
        s_copy(k).start()

    def sums(k, f, h):
        cols = k * PART + f * LANES
        return gate_acc[h * HALF : (h + 1) * HALF, cols : cols + LANES]

    def for_chip(k):
        gate_acc[:, k * PART : (k + 1) * PART] = contrib(order[k], c)

    def add_sibling(k):
        s_copy(k).wait_recv()
        here = slice(k * PART, (k + 1) * PART)
        gate_acc[:, here] = gate_acc[:, here] + sib_in[k].astype(F32)

    def send_direct(f, h):
        dir_out[f, h] = sums(1 + h, f, h).astype(BF16)
        r_copy(f, 2 + h).start()

    def send_final(f):
        for h in range(2):
            r_copy(f, h).wait_recv()
            fin_out[f, h] = (sums(2 - h, f, h) + rel_in[f, h].astype(F32)).astype(BF16)
            r_copy(f, 4 + h).start()

    for_sibling(0)
    for_sibling(1)
    for_chip(0)
    add_sibling(0)
    for f in range(2):
        for h in range(2):
            rel_out[f, h] = sums(0, f, h).astype(BF16)
            r_copy(f, h).start()
    for_sibling(2)
    for_chip(1)
    add_sibling(1)
    send_direct(0, 0)
    for_chip(2)
    add_sibling(2)
    send_direct(0, 1)

    def score_rows(i, carry):
        rows = pl.ds(pl.multiple_of(i * 16, 16), 16)
        prod = hidden[rows, :].astype(F32) * back_acc[rows, :]
        part = prod[:, 0:128]
        for j in range(1, HID // 128):
            part = part + prod[:, j * 128 : (j + 1) * 128]
        back_acc[rows, 0:128] = part
        return carry

    def q_copy(peer, place):
        return pltpu.make_async_remote_copy(
            src_ref=score_buf.at[ex], dst_ref=score_buf.at[place], send_sem=q_send.at[peer], recv_sem=q_recv.at[place],
            device_id=(seq, peer), device_id_type=MESH,
        )

    send_final(0)
    send_direct(1, 0)
    send_direct(1, 1)
    for_sibling(3)
    send_final(1)
    for_chip(3)
    lax.fori_loop(0, CAP // 16, score_rows, 0, unroll=2)
    score_part = jnp.sum(back_acc[:, 0:128].T, axis=0, keepdims=True)
    score_buf[ex] = score_part
    each_part(lambda peer: q_copy(peer, ex).start())

    def weight_rows(xx):
        def body(n):
            cols = slice(n * WIDE, (n + 1) * WIDE)
            here = pl.ds(pl.multiple_of(xx * WIDE, WIDE), WIDE)
            grad_gate[here, cols] = dot(rows_t[xx], ggp[:, cols]).astype(BF16)
            grad_up[here, cols] = dot(rows_t[xx], gup[:, cols]).astype(BF16)

        for n in range(HID // WIDE):
            body(n)

    def c_copy(f, peer, place):
        return pltpu.make_async_remote_copy(
            src_ref=out_r.at[f, slot(peer), :],
            dst_ref=in_r.at[f, slot(place), :],
            send_sem=c_send.at[f, peer],
            recv_sem=c_recv.at[f, place],
            device_id=(peer, ex),
            device_id_type=MESH,
        )

    def give_back(f):
        for k in (2, 3, 4, 5):
            r_copy(f, k).wait_recv()
        halves = [
            (sums(3, f, h) + fin_in[f, h].astype(F32) + dir_in[f, h].astype(F32)).astype(BF16) for h in range(2)
        ]
        out_r[f] = dot(pick_t[...], jnp.concatenate(halves, axis=0)).astype(BF16)
        each_peer(lambda peer: c_copy(f, peer, seq).start())
        in_r[f, slot(seq), :] = out_r[f, slot(seq), :]

    add_sibling(3)
    weight_rows(x)
    give_back(0)
    weight_rows(left)
    give_back(1)
    weight_rows(right)
    weight_rows(opp)
    hidden_t[...] = hidden[...].T
    for xx in range(CHIPS):
        scale(xx)

    each_peer(lambda peer: [x_copy(ch, peer, seq).wait_send() for ch in range(4)])
    each_part(lambda peer: q_copy(peer, ex).wait_send())
    for ch in range(4):
        for k in range(7):
            g_copy(ch, k).wait_send()
    for k in range(4):
        s_copy(k).wait_send()
    for f in range(2):
        for k in range(6):
            r_copy(f, k).wait_send()

    each_part(lambda peer: q_copy(peer, peer).wait_recv())
    total = score_buf[0]
    for i in range(1, 8):
        total = total + score_buf[i]
    score_out[...] = total

    for f in range(2):
        each_peer(lambda peer: c_copy(f, peer, peer).wait_recv())
        tok_out[:, f * LANES : (f + 1) * LANES] = dot(send_t[...], in_r[f]).astype(BF16)

    each_peer(lambda peer: [c_copy(f, peer, seq).wait_send() for f in range(2)])


def store_kernel(
    tok, score, grad_gate, grad_up, hidden_t, scaled, tok_hbm, score_hbm, gate_hbm, up_hbm, down_hbm, stage, sems
):
    copies = [
        pltpu.make_async_copy(tok, tok_hbm, sems.at[0]),
        pltpu.make_async_copy(score, score_hbm, sems.at[1]),
    ]
    for src, dst in ((grad_gate, gate_hbm), (grad_up, up_hbm)):
        for i in range(CHIPS):
            here = pl.ds(i * WIDE, WIDE)
            copies.append(pltpu.make_async_copy(src.at[here, :], dst.at[here, :], sems.at[len(copies)]))
    for copy in copies:
        copy.start()
    for i in range(CHIPS):

        def body(n, carry):
            here = pl.ds(pl.multiple_of(n * WIDE, WIDE), WIDE)
            stage[i, here, :] = dot(hidden_t[here, :], scaled[i]).astype(BF16)
            return carry

        lax.fori_loop(0, HID // WIDE, body, 0)
        last = pltpu.make_async_copy(stage.at[i], down_hbm.at[:, pl.ds(i * WIDE, WIDE)], sems.at[len(copies)])
        last.start()
        copies.append(last)
    for copy in copies:
        copy.wait()


def shards(tokens, grad_out, chosen, scores, gate_weight, up_weight, down_weight):
    vmem = pl.BlockSpec(memory_space=pltpu.VMEM)
    anyw = pl.BlockSpec(memory_space=pl.ANY)
    shape = jax.ShapeDtypeStruct
    dma = pltpu.SemaphoreType.DMA
    first = (((CAP, PART), BF16), ((1, CAP), F32), ((CHIPS * WIDE, HID), BF16), ((CHIPS * WIDE, HID), BF16))
    left_over = (((HID, CAP), BF16), ((CHIPS, CAP, WIDE), BF16))
    results = first + (((HID, CHIPS * WIDE), BF16),)
    kept = pl.pallas_call(
        layer_kernel,
        out_shape=tuple(pltpu.VMEM(*r) for r in first + left_over),
        in_specs=[vmem] * 4 + [anyw] * 3,
        out_specs=(vmem,) * 6,
        scratch_shapes=[
            pltpu.VMEM((CHIPS, WIDE, HID), BF16),
            pltpu.VMEM((CHIPS, WIDE, HID), BF16),
            pltpu.VMEM((CHIPS, HID, WIDE), BF16),
            pltpu.VMEM((2, CHIPS, CAP, WIDE), BF16),
            pltpu.VMEM((CAP, HID), F32),
            pltpu.VMEM((CAP, HID), F32),
            pltpu.VMEM((CAP, HID), F32),
            pltpu.VMEM((CAP, HID), BF16),
            pltpu.VMEM((CAP, HID), BF16),
            pltpu.VMEM((CAP, HID), BF16),
            pltpu.VMEM((CHIPS, WIDE, CAP), BF16),
            pltpu.VMEM((OWNERS * MOST, CAP), BF16),
            pltpu.VMEM((CAP, OWNERS * MOST), BF16),
            pltpu.VMEM((CAP, OWNERS * MOST), BF16),
            pltpu.VMEM((OWNERS * MOST, CAP), BF16),
            pltpu.VMEM((4, OWNERS * MOST, LANES), BF16),
            pltpu.VMEM((4, OWNERS * MOST, LANES), BF16),
            pltpu.VMEM((2, OWNERS * MOST, LANES), BF16),
            pltpu.VMEM((2, OWNERS * MOST, LANES), BF16),
            pltpu.VMEM((CHIPS, CAP, PART), BF16),
            pltpu.VMEM((CHIPS, CAP, PART), BF16),
        ]
        + [pltpu.VMEM((2, 2, HALF, LANES), BF16)] * 6
        + [
            pltpu.VMEM((8, 1, CAP), F32),
            pltpu.VMEM((CAP, 128), F32),
            dma((2 + CHIPS,)),
            dma((4, OWNERS)),
            dma((4, OWNERS)),
            dma((4, 7)),
            dma((4, 7)),
            dma((4,)),
            dma((4,)),
            dma((2, OWNERS)),
            dma((2, OWNERS)),
            dma((2, 6)),
            dma((2, 6)),
            dma((8,)),
            dma((8,)),
        ],
        compiler_params=pltpu.CompilerParams(
            collective_id=0, has_side_effects=True, vmem_limit_bytes=VMEM_BYTES
        ),
        name="layer",
    )(
        tokens,
        grad_out,
        chosen,
        scores,
        gate_weight.reshape(CHIPS, WIDE, HID),
        up_weight.reshape(CHIPS, WIDE, HID),
        down_weight,
    )
    tok, score, grad_gate, grad_up, grad_down = pl.pallas_call(
        store_kernel,
        out_shape=tuple(shape(*r) for r in results),
        in_specs=[vmem] * 6,
        out_specs=(anyw,) * 5,
        scratch_shapes=[pltpu.VMEM((CHIPS, HID, WIDE), BF16), dma((16,))],
        compiler_params=pltpu.CompilerParams(vmem_limit_bytes=8 * 1024 * 1024),
        name="store",
    )(*[pltpu.with_memory_space_constraint(k, pltpu.VMEM) for k in kept])
    return tok, score, grad_gate[None], grad_up[None], grad_down[None]


def solution(mesh):
    in_specs = (
        P("seq", "exp"),
        P("seq", "exp"),
        P(),
        P("seq", None),
        P("seq", None, "exp"),
        P("seq", None, "exp"),
        P("seq", "exp", None),
    )
    out_specs = (
        P("seq", "exp"),
        P("seq", None),
        P("seq", None, "exp"),
        P("seq", None, "exp"),
        P("seq", "exp", None),
    )
    return jax.shard_map(shards, mesh=mesh, in_specs=in_specs, out_specs=out_specs, check_vma=False)
```
